32 devices in a mesh: row: 8 (over z, y), col: 4 (over x, core).
Axes of the slice: x: 2, y: 2, z: 4, core: 2. Of those that a mesh axis runs over, the one named last changes fastest.
Arguments:
- panel_block: float32 [16384, 128], P('row', 'col'), may hold values from -6 to 6
- trailing: float32 [16384, 2048], P('row', 'col'), may hold values from -6 to 6
Outputs:
- updated: float32 [16384, 2048], P('row', 'col')
- reflectors: float32 [16384, 128], P('row', 'col')
- panel_factor: float32 [128, 128], replicated
The draws below stay inside these ranges and needn't reach their ends.
All inputs are finite; a program needn't handle non-finite values.
Results may differ from the reference program's by a relative error of at most 0.0003.
Values sent between devices are 32-bit elements; how exact they have to be, the bound alone decides.
No kernel may reach another device: no remote copies, remote signals or barrier semaphores. Data moves between devices by JAX's collectives and lax.ppermute only.
A program may use at most 64 MiB of HBM per device.

```python
import jax
import jax.numpy as jnp
from jax import lax

B = 128
M = 16384
NC = 2048


def block_scale(rng, shape, pieces, smallest, largest):
    def one(position, parts):
        heights = jax.random.uniform(jax.random.fold_in(jax.random.fold_in(rng, 6), position), (parts,), jnp.float32, smallest / len(pieces), largest / len(pieces))
        return jnp.repeat(jnp.exp(heights), shape[position] // parts).reshape((-1,) + (1,) * (len(shape) - position - 1))

    factor_of = one(*pieces[0])
    for cut in pieces[1:]:
        factor_of = factor_of * one(*cut)
    return factor_of


def scatter_about(key, shape, scale, bound, split=(), held_as=jnp.bfloat16):
    array = jax.random.normal(key, shape, jnp.float32) * scale
    if len(split) > 0:
        array = block_scale(key, shape, split, -0.22, 0.18) * array
    return jnp.clip(array, min=-bound, max=bound).astype(held_as)


def setup_inputs(seed: int = 0) -> dict:
    keys = jax.random.split(jax.random.key(seed), 3)
    return {
        "panel_block": scatter_about(keys[0], (M, B), 1.0, 6.0, ((0, 8), (1, 4)), jnp.float32),
        "trailing": scatter_about(keys[1], (M, NC), 1.0, 6.0, ((0, 8), (1, 4)), jnp.float32),
    }


HIGH = lax.Precision.HIGHEST

def decompose(matrix):
    extent = matrix.shape[0]
    positions = jnp.arange(extent)

    def advance(column, current):
        row_pick = lax.dynamic_index_in_dim(current, column, 0, keepdims=False)
        col_pick = lax.dynamic_index_in_dim(current, column, 1, keepdims=False)
        pivot_value = lax.dynamic_index_in_dim(row_pick, column, 0, keepdims=False)
        below_mask = positions > column
        factor_col = jnp.where(below_mask, col_pick / pivot_value, jnp.float32(0.0))
        current = current - factor_col[:, None] * jnp.where(below_mask, row_pick, jnp.float32(0.0))[None, :]
        place_mask = (positions == column)[None, :] & below_mask[:, None]
        return jnp.where(place_mask, factor_col[:, None], current)
    return lax.fori_loop(0, extent, advance, matrix)

def reference(panel_block, trailing):
    width = panel_block.shape[1]
    gram_full = lax.dot_general(panel_block.astype(jnp.float32), panel_block.astype(jnp.float32), (((0,), (0,)), ((), ())), precision=HIGH, preferred_element_type=jnp.float32)
    factor = jnp.linalg.cholesky(gram_full).T
    q_trans = jax.scipy.linalg.solve_triangular(factor.T, panel_block.T, lower=True)
    leading = q_trans[:, :width].T
    sign_flip = jnp.where(jnp.diag(leading) >= 0, jnp.float32(-1.0), jnp.float32(1.0))
    packed_lu = decompose(leading - jnp.diag(sign_flip))
    lower_f = jnp.tril(packed_lu, -1) + jnp.eye(width, dtype=jnp.float32)
    upper_f = jnp.triu(packed_lu)
    reflect_t = jax.scipy.linalg.solve_triangular(upper_f.T, q_trans, lower=True)
    reflect_t = reflect_t.at[:, :width].set(lower_f.T)
    coupling_t = jax.scipy.linalg.solve_triangular(lower_f, -(sign_flip[:, None] * upper_f.T), lower=True, unit_diagonal=True)
    products = lax.dot_general(trailing.astype(jnp.float32), reflect_t.astype(jnp.float32), (((0,), (1,)), ((), ())), precision=HIGH, preferred_element_type=jnp.float32)
    mixed = lax.dot_general(products.astype(jnp.float32), coupling_t.astype(jnp.float32), (((1,), (1,)), ((), ())), precision=HIGH, preferred_element_type=jnp.float32)
    change = lax.dot_general(reflect_t.astype(jnp.float32), mixed.astype(jnp.float32), (((0,), (1,)), ((), ())), precision=HIGH, preferred_element_type=jnp.float32)
    updated = trailing - change
    return (updated, reflect_t.T, sign_flip[:, None] * factor)
```

```python
import jax
import jax.numpy as jnp
from jax import lax
from jax.experimental import pallas as pl
from jax.experimental.pallas import tpu as pltpu
from jax.sharding import PartitionSpec as P

SUB = 8


def factor_kernel(gram_ref, lead_t_ref, panel_factor_ref, weight_ref, inv_ref, pivot_ref, lead_ref, g, z, d, e, lead):
    n = gram_ref.shape[0]
    slabs = n // SUB
    sub = lax.broadcasted_iota(jnp.int32, (SUB, n), 0)
    lane = lax.broadcasted_iota(jnp.int32, (SUB, n), 1)

    def rows(s):
        return pl.ds(s * SUB, SUB)

    def spread(block, j):
        return jnp.broadcast_to(block[j : j + 1, :], block.shape)

    def column(block, k):
        return jnp.broadcast_to(block[:, k : k + 1], block.shape)

    g[...] = gram_ref[...]
    d[...] = lead_t_ref[...]
    lead[...] = lead_t_ref[...].T
    for s in range(slabs):
        unit = jnp.where(sub + s * SUB == lane, 1.0, 0.0).astype(jnp.float32)
        z[rows(s), :] = unit
        e[rows(s), :] = unit

    def reduce_slab(s, left, right):
        x, y = left[rows(s), :], right[rows(s), :]
        cols = [column(x, s * SUB + j) for j in range(SUB)]
        x_at, y_at, pivots = x, y, cols[0]
        for j in range(SUB):
            here = sub == j
            pivot = spread(cols[j], j)
            inv = 1.0 / pivot
            if j > 0:
                x_at, y_at = jnp.where(here, x, x_at), jnp.where(here, y, y_at)
            pivots = jnp.where(here, pivot, pivots)
            mult = cols[j]
            xj, yj = spread(x, j) * inv, spread(y, j) * inv
            for c in range(j + 1, SUB):
                cj = spread(cols[c], j) * inv
                cols[c] = jnp.where(here, cj, cols[c] - mult * cj)
            x = jnp.where(here, xj, x - mult * xj)
            y = jnp.where(here, yj, y - mult * yj)
        return x, y, x_at, y_at, pivots

    def eliminate(s, t, left, right, xs, ys):
        x, y = left[rows(t), :], right[rows(t), :]
        cols = [column(x, s * SUB + j) for j in range(SUB)]
        for j in range(SUB):
            x = x - cols[j] * xs[j]
            y = y - cols[j] * ys[j]
        left[rows(t), :] = x
        right[rows(t), :] = y

    def cholesky(s):
        x, y, x_at, y_at, pivots = reduce_slab(s, g, z)
        scale = lax.rsqrt(pivots)
        xs = [spread(x, j) for j in range(SUB)]
        ys = [spread(y, j) for j in range(SUB)]
        for t in range(s + 1, slabs):
            eliminate(s, t, g, z, xs, ys)
        r = jnp.where(lane >= sub + s * SUB, x_at * scale, 0.0)
        r_inv_t = y_at * scale
        diagonal = jnp.sum(lead[rows(s), :] * r_inv_t, axis=1, keepdims=True)
        sign = jnp.broadcast_to(jnp.where(diagonal >= 0, -1.0, 1.0).astype(jnp.float32), (SUB, n))
        signed = sign * r
        panel_factor_ref[rows(s), :] = signed
        weight_ref[rows(s), :] = sign * r_inv_t
        turned = jnp.concatenate([signed, jnp.zeros((n - SUB, n), jnp.float32)], axis=0).T
        for t in range(s, slabs):
            part = turned[t * SUB : (t + 1) * SUB, :]
            if s:
                part = pltpu.roll(part, s * SUB, 1)
            d[rows(t), :] = d[rows(t), :] - part

    def lower_upper(s):
        x, y, _, y_at, pivots = reduce_slab(s, d, e)
        pivot_ref[rows(s), :] = y_at / pivots
        d[rows(s), :] = x
        e[rows(s), :] = y
        xs = [spread(x, j) for j in range(SUB)]
        ys = [spread(y, j) for j in range(SUB)]
        for t in list(range(s + 1, slabs)) + list(range(s)):
            eliminate(s, t, d, e, xs, ys)

    for s in range(slabs):
        cholesky(s)
        if s:
            lower_upper(s - 1)
    lower_upper(slabs - 1)
    inv_ref[...] = e[...]
    lead_ref[...] = lead_t_ref[...] - panel_factor_ref[...].T


def factor(gram, lead_t):
    n = gram.shape[0]
    out = jax.ShapeDtypeStruct((n, n), jnp.float32)
    return pl.pallas_call(
        factor_kernel,
        out_shape=(out,) * 5,
        scratch_shapes=[pltpu.VMEM((n, n), jnp.float32)] * 5,
        name="factor",
    )(gram, lead_t)


def swap(x, axis, mask):
    return lax.ppermute(x, axis, [(i, i ^ mask) for i in range(lax.axis_size(axis))])


def bits_of(axis):
    return [1 << b for b in range(lax.axis_size(axis).bit_length() - 1)]


def total(x, axis):
    for bit in bits_of(axis):
        x = x + swap(x, axis, bit)
    return x


def from_first(x, axis):
    size, me = lax.axis_size(axis), lax.axis_index(axis)
    for bit in reversed(bits_of(axis)):
        got = lax.ppermute(x, axis, [(i, i + bit) for i in range(0, size, 2 * bit)])
        x = jnp.where(me & bit != 0, got, x)
    return x


def gram_kernel(masks, me_ref, *refs):
    pieces, panel_t, gram = refs[: len(masks)], refs[-2], refs[-1]
    width = pieces[0].shape[0]
    for mask, piece in zip(masks, pieces):
        at = pl.multiple_of((me_ref[0] ^ mask) * width, width)
        panel_t[pl.ds(at, width), :] = piece[...]
    whole = panel_t[...]
    gram[...] = lax.dot_general(
        whole,
        whole,
        (((1,), (1,)), ((), ())),
        precision=lax.Precision.HIGHEST,
        preferred_element_type=jnp.float32,
    )


def gathered(own):
    held = {0: own}
    for bit in reversed(bits_of("col")):
        held.update({mask | bit: swap(piece, "col", bit) for mask, piece in list(held.items())})
    masks = tuple(held)
    width, rows = own.shape
    n = width * len(masks)
    me = lax.axis_index("col").astype(jnp.int32).reshape(1)
    return pl.pallas_call(
        lambda *refs: gram_kernel(masks, *refs),
        out_shape=(
            jax.ShapeDtypeStruct((n, rows), jnp.float32),
            jax.ShapeDtypeStruct((n, n), jnp.float32),
        ),
        in_specs=[pl.BlockSpec(memory_space=pltpu.SMEM)]
        + [pl.BlockSpec(memory_space=pltpu.VMEM)] * len(masks),
        name="gram",
    )(me, *held.values())


def dot(a, b, over, precision):
    return lax.dot_general(
        a, b, (((over[0],), (over[1],)), ((), ())), precision=precision, preferred_element_type=jnp.float32
    )


HIGHEST, HIGH = lax.Precision.HIGHEST, lax.Precision.HIGH


def per_device(panel_block, trailing):
    own = panel_block.T
    panel_t, gram_here = gathered(own)
    n = panel_t.shape[0]
    gram = total(gram_here, "row")
    lead_t = from_first(panel_t[:, :n], "row")
    lead_trailing = from_first(trailing[:n], "row")
    products = total(dot(panel_t, trailing, (1, 0), HIGH), "row")
    panel_factor, weight, inv_t, pivot_t, replaced = factor(gram, lead_t)
    rest = lead_trailing - dot(weight, products, (1, 0), HIGHEST)
    mixed = dot(inv_t, rest, (0, 0), HIGHEST)
    first = lax.axis_index("row") == 0
    panel_t = panel_t.at[:, :n].set(jnp.where(first, replaced, panel_t[:, :n]))
    updated = trailing - dot(panel_t, mixed, (0, 0), HIGH)
    width = own.shape[0]
    pivot_part = lax.dynamic_slice_in_dim(pivot_t, lax.axis_index("col") * width, width, 0)
    reflectors = dot(pivot_part, panel_t, (1, 0), HIGH)
    return updated, reflectors.T, panel_factor


def solution(mesh):
    in_specs = (P("row", "col"), P("row", "col"))
    out_specs = (P("row", "col"), P("row", "col"), P())
    return jax.shard_map(per_device, mesh=mesh, in_specs=in_specs, out_specs=out_specs, check_vma=False)
```

```python
import jax
import jax.numpy as jnp
from jax import lax
from jax.experimental import pallas as pl
from jax.experimental.pallas import tpu as pltpu
from jax.sharding import PartitionSpec as P

SUB = 16
GROUP = 2
LAG = 2
HIGHEST, HIGH = lax.Precision.HIGHEST, lax.Precision.HIGH
MOST = 60 << 20
MOST = 50 << 20
FREE = pl.CostEstimate(flops=1, bytes_accessed=1, transcendentals=0)
SCALAR = pl.BlockSpec(memory_space=pltpu.SMEM)
WHOLE = pl.BlockSpec(memory_space=pltpu.VMEM)


def dot(a, b, over, precision=HIGHEST):
    return lax.dot_general(
        a, b, (((over[0],), (over[1],)), ((), ())), precision=precision, preferred_element_type=jnp.float32
    )


def interleave(streams):
    steps = [((i + 0.5) / len(stream), k, step) for k, stream in enumerate(streams) for i, step in enumerate(stream)]
    for _, _, step in sorted(steps, key=lambda item: item[:2]):
        step()


def factor_kernel(even_ref, mine_ref, theirs_ref, panel_factor_ref, weight_ref, inv_ref, pivot_ref, replaced_ref, g, d, lower, upper, lead_ref):
    n = mine_ref.shape[0]
    slabs = n // SUB
    sub = lax.broadcasted_iota(jnp.int32, (SUB, n), 0)
    lane = lax.broadcasted_iota(jnp.int32, (SUB, n), 1)
    one = jnp.float32(1.0)
    state = {}

    def rows(s):
        return pl.ds(s * SUB, SUB)

    def spread(block, j):
        return jnp.broadcast_to(block[j : j + 1, :], block.shape)

    def columns(block, s):
        return [jnp.broadcast_to(block[:, k : k + 1], block.shape) for k in range(s * SUB, (s + 1) * SUB)]

    def within(first, last):
        return (lane >= first * SUB) & (lane < last * SUB)

    def group(s):
        first = s // GROUP * GROUP
        return range(first, first + GROUP)

    def reduce_steps(name, s, ref):
        me = state[name, s] = {}
        split = name == "g"

        def begin():
            block = ref[rows(s), :]
            unit = jnp.where(sub + s * SUB == lane, one, 0.0)
            me["cols"] = columns(block, s)
            if split:
                me["arrays"] = [block, jnp.where(lane < s * SUB, block, unit)]
                me["at"] = list(me["arrays"])
            else:
                me["arrays"] = [jnp.where(within(s, s + 1), unit, block)]
                me["upper"] = unit

        def step(j):
            here = sub == j
            cols = me["cols"]
            inv = 1.0 / spread(cols[j], j)
            me["inv"] = inv if j == 0 else jnp.where(here, inv, me["inv"])
            if j and split:
                me["at"] = [jnp.where(here, a, b) for a, b in zip(me["arrays"], me["at"])]
            mult = jnp.where(here, 0.0, cols[j]) * inv
            for c in range(j + 1, SUB):
                cols[c] = cols[c] - mult * spread(cols[c], j)
            me["arrays"] = [a - mult * spread(a, j) for a in me["arrays"]]
            if j and not split:
                me["upper"] = me["upper"] - jnp.where(sub < j, mult, 0.0) * spread(me["upper"], j)

        def end():
            scaled = [a * me["inv"] for a in me["arrays"]]
            whole = jnp.where(lane < (s + 1) * SUB, scaled[1], scaled[0]) if split else scaled[0]
            me["rows"] = [spread(whole, j) for j in range(SUB)]
            ref[rows(s), :] = whole
            if not split:
                full = me["upper"] * me["inv"]
                me["upper_rows"] = [spread(full, j) for j in range(SUB)]
                upper[rows(s), :] = full

        return [begin] + [lambda j=j: step(j) for j in range(SUB)] + [end]

    def eliminate(name, s, t, ref):
        def run():
            block = ref[rows(t), :]
            cols = columns(block, s)
            block = jnp.where(within(s, s + 1), 0.0, block)
            for col, row in zip(cols, state[name, s]["rows"]):
                block = block - col * row
            ref[rows(t), :] = block
            if name == "d" and t < s:
                block = upper[rows(t), :]
                for col, row in zip(cols, state[name, s]["upper_rows"]):
                    block = block - col * row
                upper[rows(t), :] = block

        return run

    def times(a, b):
        return jnp.dot(a, b, precision=lax.Precision.HIGHEST, preferred_element_type=jnp.float32)

    def others(name, s, ref):
        first, last = group(s)[0], group(s)[-1] + 1

        def run():
            whole = ref[...]
            mask = within(first, last)
            if name == "g":
                targets = list(range(last, slabs))
                left = jnp.concatenate([jnp.where(mask, whole[t * SUB : (t + 1) * SUB], 0.0) for t in targets], axis=0)
                change = times(left, whole)
            else:
                targets = list(range(slabs))
                left = jnp.concatenate(
                    [
                        jnp.where(mask, lower[rows(t), :] if t in group(s) else whole[t * SUB : (t + 1) * SUB], 0.0)
                        for t in targets
                    ],
                    axis=0,
                )
                change = times(left, whole)
                below = times(left[first * SUB :], upper[...])
                for i, t in enumerate(range(first, slabs)):
                    part = below[i * SUB : (i + 1) * SUB]
                    lower[rows(t), :] = jnp.where(mask, part, jnp.where(lane < first * SUB, lower[rows(t), :], 0.0))
            for i, t in enumerate(targets):
                if t not in group(s):
                    block = jnp.where(mask, 0.0, whole[t * SUB : (t + 1) * SUB])
                    ref[rows(t), :] = block - change[i * SUB : (i + 1) * SUB]

        return run

    started = set()

    def start_group(s):
        for t in group(s):
            lower[rows(t), :] = jnp.where(lane < s * SUB, lower[rows(t), :], d[rows(t), :]) if s else d[rows(t), :]
            started.add(t)

    def cholesky_out(s):
        me = state["g", s]

        def first():
            scale = jnp.sqrt(me["inv"])
            x_at, y_at = me["at"]
            me["r"] = jnp.where(lane >= sub + s * SUB, x_at * scale, 0.0)
            me["r_inv_t"] = y_at * scale
            diagonal = jnp.sum(lead_ref[rows(s), :] * me["r_inv_t"], axis=1, keepdims=True)
            me["sign"] = jnp.broadcast_to(jnp.where(diagonal >= 0, -one, one), (SUB, n))

        def second():
            signed = me["sign"] * me["r"]
            panel_factor_ref[rows(s), :] = signed
            weight_ref[rows(s), :] = me["sign"] * me["r_inv_t"]
            replaced_ref[rows(s), :] = lead_ref[rows(s), :] - signed
            d[rows(s), :] = d[rows(s), :] - signed
            if s in started:
                lower[rows(s), :] = lower[rows(s), :] - signed

        return [first, second]

    even = even_ref[0] == 0
    g[...] = jnp.where(even, mine_ref[...], theirs_ref[...])
    lead_ref[...] = jnp.where(even, theirs_ref[...], mine_ref[...])
    d[...] = lead_ref[...]
    lower[...] = jnp.zeros((n, n), jnp.float32)
    upper[...] = jnp.zeros((n, n), jnp.float32)
    for k in range(slabs + LAG):
        streams, after = [], []
        if 0 <= k - 1 < slabs:
            streams.append(cholesky_out(k - 1))
        for name, s, ref in (("g", k, g), ("d", k - LAG, d)):
            if not 0 <= s < slabs:
                continue
            if name == "d" and s % GROUP == 0:
                start_group(s)
            if s % GROUP:
                streams.append([eliminate(name, s - 1, t, ref) for t in group(s) if t not in (s - 1, s)])
            chain = reduce_steps(name, s, ref)
            if (s + 1) % GROUP:
                chain.append(eliminate(name, s, s + 1, ref))
            else:
                chain += [eliminate(name, s, t, ref) for t in group(s) if t != s]
                if name == "d" or s + 1 < slabs:
                    after.append(others(name, s, ref))
            streams.append(chain)
        interleave([s for s in streams if s])
        for step in after:
            step()
    inv_ref[...] = d[...]
    pivot_ref[...] = times(d[...], lower[...])


def factor(odd, mine, theirs):
    n = mine.shape[0]
    out = jax.ShapeDtypeStruct((n, n), jnp.float32)
    return pl.pallas_call(
        factor_kernel,
        out_shape=(out,) * 5,
        in_specs=[SCALAR, WHOLE, WHOLE],
        scratch_shapes=[pltpu.VMEM((n, n), jnp.float32)] * 5,
        compiler_params=pltpu.CompilerParams(vmem_limit_bytes=4 << 20),
        cost_estimate=FREE,
        name="factor",
    )(odd, mine, theirs)


def swap(x, axis, mask):
    return lax.ppermute(x, axis, [(i, i ^ mask) for i in range(lax.axis_size(axis))])


def bits_of(axis):
    return [1 << b for b in range(lax.axis_size(axis).bit_length() - 1)]


def halves(x):
    high = x.astype(jnp.bfloat16)
    return high, (x - high.astype(jnp.float32)).astype(jnp.bfloat16)


def anywhere():
    return pl.BlockSpec(memory_space=pl.ANY)


def fetch(trailing, held, got, steps=4):
    tall = trailing.shape[0] // steps
    copies = [
        pltpu.make_async_copy(trailing.at[pl.ds(i * tall, tall)], held.at[pl.ds(i * tall, tall)], got.at[i])
        for i in range(steps)
    ]
    for copy in copies:
        copy.start()
    return copies


def product(pieces, held, copies):
    left = jnp.concatenate([piece[...] for piece in pieces], axis=0)
    high, low = halves(left)
    both = jnp.concatenate([high, low], axis=0)
    m, tall = left.shape[0], held.shape[0] // len(copies)
    sums = jnp.zeros((m, held.shape[1]), jnp.float32)
    for i, copy in enumerate(copies):
        copy.wait()
        right_high, right_low = halves(held[i * tall : (i + 1) * tall, :])
        part = slice(i * tall, (i + 1) * tall)
        one = jnp.dot(both[:, part], right_high, preferred_element_type=jnp.float32)
        two = jnp.dot(high[:, part], right_low, preferred_element_type=jnp.float32)
        sums = sums + (one[:m] + one[m:] + two)
    return sums


def near_kernel(*refs):
    *pieces, trailing, out, held, got = refs
    out[...] = product(pieces, held, fetch(trailing, held, got))


def near_products(pieces, trailing):
    m, cols = sum(p.shape[0] for p in pieces), trailing.shape[1]
    return pl.pallas_call(
        near_kernel,
        out_shape=jax.ShapeDtypeStruct((m, cols), jnp.float32),
        in_specs=[WHOLE] * len(pieces) + [anywhere()],
        scratch_shapes=[pltpu.VMEM(trailing.shape, jnp.float32), pltpu.SemaphoreType.DMA((4,))],
        compiler_params=pltpu.CompilerParams(vmem_limit_bytes=MOST),
        cost_estimate=FREE,
        name="products",
    )(*pieces, trailing)


def gram_kernel(masks, near, where_ref, *refs):
    pieces, others = refs[: len(masks)], refs[len(masks) :]
    near_sums, trailing, panel_t, mine, keep, give, sums, held, got = others
    copies = fetch(trailing, held, got)
    col, row = where_ref[0], where_ref[1]
    width = pieces[0].shape[0]
    n = width * len(masks)

    def at(mask):
        return pl.ds(pl.multiple_of((col ^ mask) * width, width), width)

    for mask, piece in zip(masks, pieces):
        panel_t[at(mask), :] = piece[...]

    @pl.when(col & 1 == 0)
    def _():
        whole = panel_t[...]
        mine[...] = dot(whole, whole, (1, 1))

    @pl.when(col & 1 == 1)
    def _():
        mine[...] = jnp.where(row == 0, panel_t[:, :n].T, 0.0)

    far = [(mask, piece) for mask, piece in zip(masks, pieces) if mask not in near]
    late = product([piece for _, piece in far], held, copies)
    for i, mask in enumerate(near):
        sums[at(mask), :] = near_sums[i * width : (i + 1) * width, :]
    for i, (mask, _) in enumerate(far):
        sums[at(mask), :] = late[i * width : (i + 1) * width, :]
    half = sums.shape[1] // 2
    first = row & 1 == 0
    keep[...] = jnp.where(first, sums[:, :half], sums[:, half:])
    give[...] = jnp.where(first, sums[:, half:], sums[:, :half])


def gram(where, held, near, near_sums, trailing):
    width, rows = held[0].shape
    n, cols = width * len(held), trailing.shape[1]
    part = jax.ShapeDtypeStruct((n, cols // 2), jnp.float32)
    return pl.pallas_call(
        lambda *refs: gram_kernel(tuple(held), near, *refs),
        out_shape=(
            jax.ShapeDtypeStruct((n, rows), jnp.float32),
            jax.ShapeDtypeStruct((n, n), jnp.float32),
            part,
            part,
        ),
        in_specs=[SCALAR] + [WHOLE] * (len(held) + 1) + [anywhere()],
        scratch_shapes=[
            pltpu.VMEM((n, cols), jnp.float32),
            pltpu.VMEM(trailing.shape, jnp.float32),
            pltpu.SemaphoreType.DMA((4,)),
        ],
        compiler_params=pltpu.CompilerParams(vmem_limit_bytes=MOST),
        cost_estimate=FREE,
        name="gram",
    )(where, *held.values(), near_sums, trailing)


def split_kernel(panel_t, left):
    n, rows = panel_t.shape
    for i in range(0, rows, n):
        high, low = halves(panel_t[:, i : i + n].T)
        left[i : i + n, :n] = high
        left[i : i + n, n:] = low


def split_rows(panel_t):
    n, rows = panel_t.shape
    return pl.pallas_call(
        split_kernel,
        out_shape=jax.ShapeDtypeStruct((rows, 2 * n), jnp.bfloat16),
        in_specs=[WHOLE],
        compiler_params=pltpu.CompilerParams(vmem_limit_bytes=8 << 20),
        cost_estimate=FREE,
        name="split_rows",
    )(panel_t)


def update_kernel(second, where_ref, left_ref, mixed, trailing, *refs):
    if second:
        _, updated, high_ref, low_ref, result, sent = refs
    else:
        pivot, replaced, updated, reflectors, new_left, high_ref, low_ref, result, sent = refs
    row = where_ref[1]
    n, half = mixed.shape
    steps, tall = result.shape[0], result.shape[1]
    mine = row & 1 if not second else 1 - (row & 1)
    columns = pl.ds(pl.multiple_of(mine * half, half), half)
    high, low = halves(mixed[...])
    high_ref[:n], high_ref[n:] = high, high
    low_ref[:n], low_ref[n:] = low, low

    def going(i):
        return pltpu.make_async_copy(result.at[i], updated.at[pl.ds(i * tall, tall), columns], sent.at[i])

    def rows_of(i):
        left = left_ref[i * tall : (i + 1) * tall, :]
        if i == 0 and not second:
            top = jnp.concatenate(halves(replaced[...]), axis=1)
            left = jnp.concatenate([jnp.where(row == 0, top, left[:n]), left[n:]], axis=0)
            new_left[...] = left[:n]
        return left

    def times(left, high, low):
        return jnp.dot(left, high, preferred_element_type=jnp.float32) + jnp.dot(
            left, low, preferred_element_type=jnp.float32
        )

    for i in range(steps):
        result[i] = trailing[i * tall : (i + 1) * tall, columns] - times(rows_of(i), high_ref[...], low_ref[...])
        going(i).start()
    if not second:
        width = reflectors.shape[0]
        own = pivot[...]
        own = pltpu.roll(own, (n - where_ref[0] * width) % n, 1)
        a, b = halves(own)
        a, b = jnp.concatenate([a, a], axis=0), jnp.concatenate([b, b], axis=0)
        for i in range(steps):
            left = left_ref[i * tall : (i + 1) * tall, :]
            if i == 0:
                left = jnp.concatenate([new_left[...], left[n:]], axis=0)
            reflectors[:, i * tall : (i + 1) * tall] = times(left, a, b).T[:width]
    for i in range(steps):
        going(i).wait()


def update(where, left, mixed, trailing, pivot, replaced, width):
    n, half = mixed.shape
    rows, cols = trailing.shape
    steps = 4
    return pl.pallas_call(
        lambda *refs: update_kernel(False, *refs),
        out_shape=(
            jax.ShapeDtypeStruct((rows, cols), jnp.float32),
            jax.ShapeDtypeStruct((width, rows), jnp.float32),
            jax.ShapeDtypeStruct((n, 2 * n), jnp.bfloat16),
        ),
        in_specs=[SCALAR] + [WHOLE] * 5,
        out_specs=(anywhere(), WHOLE, WHOLE),
        scratch_shapes=[pltpu.VMEM((2 * n, half), jnp.bfloat16)] * 2
        + [pltpu.VMEM((steps, rows // steps, half), jnp.float32)]
        + [pltpu.SemaphoreType.DMA((steps,))],
        compiler_params=pltpu.CompilerParams(vmem_limit_bytes=8 << 20),
        cost_estimate=FREE,
        name="update",
    )(where, left, mixed, trailing, pivot, replaced)


def update_rest(where, left, new_left, mixed, trailing, updated):
    n, half = mixed.shape
    rows, cols = trailing.shape
    steps = 4

    def kernel(where_ref, left_ref, new_left_ref, mixed_ref, trailing_ref, updated_ref, *refs):
        out, scratch, high, low, result, sent = refs
        scratch[...] = left_ref[...]
        scratch[:n, :] = new_left_ref[...]
        update_kernel(True, where_ref, scratch, mixed_ref, trailing_ref, updated_ref, out, high, low, result, sent)

    return pl.pallas_call(
        kernel,
        out_shape=jax.ShapeDtypeStruct((rows, cols), jnp.float32),
        in_specs=[SCALAR] + [WHOLE] * 4 + [anywhere()],
        out_specs=anywhere(),
        scratch_shapes=[pltpu.VMEM((rows, 2 * n), jnp.bfloat16)]
        + [pltpu.VMEM((2 * n, half), jnp.bfloat16)] * 2
        + [pltpu.VMEM((steps, rows // steps, half), jnp.float32)]
        + [pltpu.SemaphoreType.DMA((steps,))],
        input_output_aliases={5: 0},
        compiler_params=pltpu.CompilerParams(vmem_limit_bytes=8 << 20),
        cost_estimate=FREE,
        name="update_rest",
    )(where, left, new_left, mixed, trailing, updated)


def mix(mine, theirs, lead, weight, inv):
    def kernel(mine, theirs, lead, weight, inv, mixed):
        rest = lead[...] - dot(weight[...], mine[...] + theirs[...], (1, 0))
        mixed[...] = dot(inv[...], rest, (1, 0))

    return pl.pallas_call(
        kernel,
        out_shape=jax.ShapeDtypeStruct(mine.shape, jnp.float32),
        in_specs=[WHOLE] * 5,
        compiler_params=pltpu.CompilerParams(vmem_limit_bytes=3 << 20),
        cost_estimate=FREE,
        name="mix",
    )(mine, theirs, lead, weight, inv)


def after(x, *others):
    return lax.optimization_barrier((x, *others))[0]


def per_device(panel_block, trailing):
    own = panel_block.T
    col, row = lax.axis_index("col"), lax.axis_index("row")
    where = jnp.stack([col, row]).astype(jnp.int32)
    held = {0: own}
    for bit in reversed(bits_of("col")):
        held.update({mask | bit: swap(piece, "col", bit) for mask, piece in list(held.items())})
    n = own.shape[0] * len(held)
    bits = bits_of("row")
    order = sorted(held)
    near, far = order[: len(order) // 2], order[len(order) // 2 :]

    odd = row & bits[0] != 0
    half = trailing.shape[1] // 2
    left_half, right_half = trailing[:n, :half], trailing[:n, half:]
    lead_got = swap(jnp.where(odd, left_half, right_half), "row", bits[0])
    lead = jnp.where(odd, lead_got, left_half)
    lead_got = swap(lead, "row", bits[-1])
    near_sums = near_products([held[m] for m in near], trailing)
    held[far[0]], near_sums, lead = lax.optimization_barrier((held[far[0]], near_sums, lead))
    for m in far[1:]:
        held[m] = swap(held[far[0]], "col", m ^ far[0])
    panel_t, mine, keep, give = gram(where, held, near, near_sums, trailing)
    left = split_rows(panel_t)
    got = swap(give, "row", bits[0])
    for bit in bits[1:-1]:
        mine = mine + swap(mine, "row", bit)
    lead_got, got, mine = lax.optimization_barrier((lead_got, got, mine))
    lead = jnp.where(row & bits[-1] != 0, lead_got, lead)
    for bit in reversed(bits[1:-1]):
        lead = jnp.where(row & bit != 0, swap(lead, "row", bit), lead)
    mine = mine + swap(mine, "row", bits[-1])
    sums, lead, _ = lax.optimization_barrier((keep + got, lead, mine))
    mine, left = lax.optimization_barrier((mine + swap(mine, "row", bits[0]), left))
    for bit in bits[1:-1]:
        sums = sums + swap(sums, "row", bit)
    theirs = swap(mine, "col", 1)
    last = swap(sums, "row", bits[-1])
    theirs, sums = lax.optimization_barrier((theirs, sums))
    panel_factor, weight, inv, pivot, replaced = factor(col.astype(jnp.int32).reshape(1) & 1, mine, theirs)
    mixed = mix(sums, last, lead, weight, inv)
    other = swap(mixed, "row", bits[0])
    updated, reflectors, top = update(where, left, mixed, trailing, pivot, replaced, own.shape[0])
    updated = update_rest(where, left, top, other, trailing, updated)
    return updated, reflectors.T, panel_factor


def solution(mesh):
    in_specs = (P("row", "col"), P("row", "col"))
    out_specs = (P("row", "col"), P("row", "col"), P())
    return jax.shard_map(per_device, mesh=mesh, in_specs=in_specs, out_specs=out_specs, check_vma=False)
```

```python
import jax
import jax.numpy as jnp
from jax import lax
from jax.experimental import pallas as pl
from jax.experimental.pallas import tpu as pltpu
from jax.sharding import PartitionSpec as P

SUB = 16
GROUP = 2
LAG = 2
HIGHEST, HIGH = lax.Precision.HIGHEST, lax.Precision.HIGH
MOST = 60 << 20
MOST = 50 << 20
FREE = pl.CostEstimate(flops=1, bytes_accessed=1, transcendentals=0)
SCALAR = pl.BlockSpec(memory_space=pltpu.SMEM)
WHOLE = pl.BlockSpec(memory_space=pltpu.VMEM)


def dot(a, b, over, precision=HIGHEST):
    return lax.dot_general(
        a, b, (((over[0],), (over[1],)), ((), ())), precision=precision, preferred_element_type=jnp.float32
    )


def interleave(streams):
    steps = [((i + 0.5) / len(stream), k, step) for k, stream in enumerate(streams) for i, step in enumerate(stream)]
    for _, _, step in sorted(steps, key=lambda item: item[:2]):
        step()


def factor_kernel(even_ref, mine_ref, theirs_ref, panel_factor_ref, weight_ref, inv_ref, pivot_ref, replaced_ref, g, d, lower, upper, lead_ref):
    n = mine_ref.shape[0]
    slabs = n // SUB
    sub = lax.broadcasted_iota(jnp.int32, (SUB, n), 0)
    lane = lax.broadcasted_iota(jnp.int32, (SUB, n), 1)
    one = jnp.float32(1.0)
    state = {}

    def rows(s):
        return pl.ds(s * SUB, SUB)

    def spread(block, j):
        return jnp.broadcast_to(block[j : j + 1, :], block.shape)

    def columns(block, s):
        return [jnp.broadcast_to(block[:, k : k + 1], block.shape) for k in range(s * SUB, (s + 1) * SUB)]

    def within(first, last):
        return (lane >= first * SUB) & (lane < last * SUB)

    def group(s):
        first = s // GROUP * GROUP
        return range(first, first + GROUP)

    def reduce_steps(name, s, ref):
        me = state[name, s] = {}
        split = name == "g"

        def begin():
            block = ref[rows(s), :]
            unit = jnp.where(sub + s * SUB == lane, one, 0.0)
            me["cols"] = columns(block, s)
            if split:
                me["arrays"] = [block, jnp.where(lane < s * SUB, block, unit)]
                me["at"] = list(me["arrays"])
            else:
                me["arrays"] = [jnp.where(within(s, s + 1), unit, block)]
                me["upper"] = unit

        def step(j):
            here = sub == j
            cols = me["cols"]
            inv = 1.0 / spread(cols[j], j)
            me["inv"] = inv if j == 0 else jnp.where(here, inv, me["inv"])
            if j and split:
                me["at"] = [jnp.where(here, a, b) for a, b in zip(me["arrays"], me["at"])]
            mult = jnp.where(here, 0.0, cols[j]) * inv
            for c in range(j + 1, SUB):
                cols[c] = cols[c] - mult * spread(cols[c], j)
            me["arrays"] = [a - mult * spread(a, j) for a in me["arrays"]]
            if j and not split:
                me["upper"] = me["upper"] - jnp.where(sub < j, mult, 0.0) * spread(me["upper"], j)

        def end():
            scaled = [a * me["inv"] for a in me["arrays"]]
            whole = jnp.where(lane < (s + 1) * SUB, scaled[1], scaled[0]) if split else scaled[0]
            me["rows"] = [spread(whole, j) for j in range(SUB)]
            ref[rows(s), :] = whole
            if not split:
                full = me["upper"] * me["inv"]
                me["upper_rows"] = [spread(full, j) for j in range(SUB)]
                upper[rows(s), :] = full

        return [begin] + [lambda j=j: step(j) for j in range(SUB)] + [end]

    def eliminate(name, s, t, ref):
        def run():
            block = ref[rows(t), :]
            cols = columns(block, s)
            block = jnp.where(within(s, s + 1), 0.0, block)
            for col, row in zip(cols, state[name, s]["rows"]):
                block = block - col * row
            ref[rows(t), :] = block
            if name == "d" and t < s:
                block = upper[rows(t), :]
                for col, row in zip(cols, state[name, s]["upper_rows"]):
                    block = block - col * row
                upper[rows(t), :] = block

        return run

    def times(a, b):
        return jnp.dot(a, b, precision=lax.Precision.HIGHEST, preferred_element_type=jnp.float32)

    def others(name, s, ref):
        first, last = group(s)[0], group(s)[-1] + 1

        def run():
            whole = ref[...]
            mask = within(first, last)
            if name == "g":
                targets = list(range(last, slabs))
                left = jnp.concatenate([jnp.where(mask, whole[t * SUB : (t + 1) * SUB], 0.0) for t in targets], axis=0)
                change = times(left, whole)
            else:
                targets = list(range(slabs))
                left = jnp.concatenate(
                    [
                        jnp.where(mask, lower[rows(t), :] if t in group(s) else whole[t * SUB : (t + 1) * SUB], 0.0)
                        for t in targets
                    ],
                    axis=0,
                )
                change = times(left, whole)
                below = times(left[first * SUB :], upper[...])
                for i, t in enumerate(range(first, slabs)):
                    part = below[i * SUB : (i + 1) * SUB]
                    lower[rows(t), :] = jnp.where(mask, part, jnp.where(lane < first * SUB, lower[rows(t), :], 0.0))
            for i, t in enumerate(targets):
                if t not in group(s):
                    block = jnp.where(mask, 0.0, whole[t * SUB : (t + 1) * SUB])
                    ref[rows(t), :] = block - change[i * SUB : (i + 1) * SUB]

        return run

    started = set()

    def start_group(s):
        for t in group(s):
            lower[rows(t), :] = jnp.where(lane < s * SUB, lower[rows(t), :], d[rows(t), :]) if s else d[rows(t), :]
            started.add(t)

    def cholesky_out(s):
        me = state["g", s]

        def first():
            scale = jnp.sqrt(me["inv"])
            x_at, y_at = me["at"]
            me["r"] = jnp.where(lane >= sub + s * SUB, x_at * scale, 0.0)
            me["r_inv_t"] = y_at * scale
            diagonal = jnp.sum(lead_ref[rows(s), :] * me["r_inv_t"], axis=1, keepdims=True)
            me["sign"] = jnp.broadcast_to(jnp.where(diagonal >= 0, -one, one), (SUB, n))

        def second():
            signed = me["sign"] * me["r"]
            panel_factor_ref[rows(s), :] = signed
            weight_ref[rows(s), :] = me["sign"] * me["r_inv_t"]
            replaced_ref[rows(s), :] = lead_ref[rows(s), :] - signed
            d[rows(s), :] = d[rows(s), :] - signed
            if s in started:
                lower[rows(s), :] = lower[rows(s), :] - signed

        return [first, second]

    even = even_ref[0] == 0
    g[...] = jnp.where(even, mine_ref[...], theirs_ref[...])
    lead_ref[...] = jnp.where(even, theirs_ref[...], mine_ref[...])
    d[...] = lead_ref[...]
    lower[...] = jnp.zeros((n, n), jnp.float32)
    upper[...] = jnp.zeros((n, n), jnp.float32)
    for k in range(slabs + LAG):
        streams, after = [], []
        if 0 <= k - 1 < slabs:
            streams.append(cholesky_out(k - 1))
        for name, s, ref in (("g", k, g), ("d", k - LAG, d)):
            if not 0 <= s < slabs:
                continue
            if name == "d" and s % GROUP == 0:
                start_group(s)
            if s % GROUP:
                streams.append([eliminate(name, s - 1, t, ref) for t in group(s) if t not in (s - 1, s)])
            chain = reduce_steps(name, s, ref)
            if (s + 1) % GROUP:
                chain.append(eliminate(name, s, s + 1, ref))
            else:
                chain += [eliminate(name, s, t, ref) for t in group(s) if t != s]
                if name == "d" or s + 1 < slabs:
                    after.append(others(name, s, ref))
            streams.append(chain)
        interleave([s for s in streams if s])
        for step in after:
            step()
    inv_ref[...] = d[...]
    pivot_ref[...] = times(d[...], lower[...])


def fetching_factor_kernel(odd, mine, theirs, trailing, *refs):
    *outs, held = refs[:6]
    *scratch, got = refs[6:]
    copy = pltpu.make_async_copy(trailing, held, got.at[0])
    copy.start()

    @pl.when(odd[0] >= 0)
    def _():
        factor_kernel(odd, mine, theirs, *outs, *scratch)

    copy.wait()


def factor(odd, mine, theirs, trailing):
    n = mine.shape[0]
    out = jax.ShapeDtypeStruct((n, n), jnp.float32)
    return pl.pallas_call(
        fetching_factor_kernel,
        out_shape=(out,) * 5 + (jax.ShapeDtypeStruct(trailing.shape, jnp.float32),),
        in_specs=[SCALAR, WHOLE, WHOLE, anywhere()],
        scratch_shapes=[pltpu.VMEM((n, n), jnp.float32)] * 5 + [pltpu.SemaphoreType.DMA((1,))],
        compiler_params=pltpu.CompilerParams(vmem_limit_bytes=47 << 20),
        cost_estimate=pl.CostEstimate(flops=0, bytes_accessed=22_000_000, transcendentals=0),
        name="factor",
    )(odd, mine, theirs, trailing)


def swap(x, axis, mask):
    return lax.ppermute(x, axis, [(i, i ^ mask) for i in range(lax.axis_size(axis))])


def bits_of(axis):
    return [1 << b for b in range(lax.axis_size(axis).bit_length() - 1)]


def halves(x):
    high = x.astype(jnp.bfloat16)
    return high, (x - high.astype(jnp.float32)).astype(jnp.bfloat16)


def anywhere():
    return pl.BlockSpec(memory_space=pl.ANY)


def fetch(trailing, held, got, steps=8):
    tall = trailing.shape[0] // steps
    copies = [
        pltpu.make_async_copy(trailing.at[pl.ds(i * tall, tall)], held.at[pl.ds(i * tall, tall)], got.at[i])
        for i in range(steps)
    ]
    for copy in copies:
        copy.start()
    return copies


def product(pieces, held, copies):
    left = jnp.concatenate([piece[...] for piece in pieces], axis=0)
    high, low = halves(left)
    both = jnp.concatenate([high, low], axis=0)
    m, tall = left.shape[0], held.shape[0] // len(copies)
    sums = jnp.zeros((m, held.shape[1]), jnp.float32)
    for i, copy in enumerate(copies):
        copy.wait()
        right_high, right_low = halves(held[i * tall : (i + 1) * tall, :])
        part = slice(i * tall, (i + 1) * tall)
        one = jnp.dot(both[:, part], right_high, preferred_element_type=jnp.float32)
        two = jnp.dot(high[:, part], right_low, preferred_element_type=jnp.float32)
        sums = sums + (one[:m] + one[m:] + two)
    return sums


def gram_kernel(masks, where_ref, *refs):
    pieces, panel_t, mine = refs[: len(masks)], refs[-2], refs[-1]
    col, row = where_ref[0], where_ref[1]
    width = pieces[0].shape[0]
    n = width * len(masks)
    for mask, piece in zip(masks, pieces):
        panel_t[pl.ds(pl.multiple_of((col ^ mask) * width, width), width), :] = piece[...]

    @pl.when(col & 1 == 0)
    def _():
        whole = panel_t[...]
        high = whole.astype(jnp.bfloat16)
        rest = whole - high.astype(jnp.float32)
        middle = rest.astype(jnp.bfloat16)
        low = (rest - middle.astype(jnp.float32)).astype(jnp.bfloat16)
        parts = lax.dot_general(
            jnp.concatenate([high, middle, low], axis=0),
            jnp.concatenate([high, middle], axis=0),
            (((1,), (1,)), ((), ())),
            preferred_element_type=jnp.float32,
        )
        small = parts[n : 2 * n, n:] + (parts[2 * n :, :n] + parts[2 * n :, :n].T)
        mine[...] = parts[:n, :n] + ((parts[n : 2 * n, :n] + parts[:n, n:]) + small)

    @pl.when(col & 1 == 1)
    def _():
        mine[...] = jnp.where(row == 0, panel_t[:, :n].T, 0.0)


def gram(where, held):
    width, rows = held[0].shape
    n = width * len(held)
    return pl.pallas_call(
        lambda *refs: gram_kernel(tuple(held), *refs),
        out_shape=(jax.ShapeDtypeStruct((n, rows), jnp.float32), jax.ShapeDtypeStruct((n, n), jnp.float32)),
        in_specs=[SCALAR] + [WHOLE] * len(held),
        compiler_params=pltpu.CompilerParams(vmem_limit_bytes=8 << 20),
        cost_estimate=FREE,
        name="gram",
    )(where, *held.values())


def copy_kernel(x, out):
    out[...] = x[...]


def nearby(x):
    return pl.pallas_call(
        copy_kernel,
        out_shape=jax.ShapeDtypeStruct(x.shape, x.dtype),
        in_specs=[WHOLE],
        compiler_params=pltpu.CompilerParams(vmem_limit_bytes=1 << 20),
        cost_estimate=FREE,
        name="nearby",
    )(x)


def products_kernel(where_ref, panel_t, trailing, keep, give, left, held, got):
    copies = fetch(trailing, held, got)
    n, rows = panel_t.shape

    @pl.when(where_ref[1] >= 0)
    def _():
        for i in range(0, rows, n):
            left[i : i + n, :n], left[i : i + n, n:] = halves(panel_t[:, i : i + n].T)
        sums = product([panel_t], held, copies)
        half = sums.shape[1] // 2
        first = where_ref[1] & 1 == 0
        keep[...] = jnp.where(first, sums[:, :half], sums[:, half:])
        give[...] = jnp.where(first, sums[:, half:], sums[:, :half])


def products_of(where, panel_t, trailing):
    (n, rows), cols = panel_t.shape, trailing.shape[1]
    part = jax.ShapeDtypeStruct((n, cols // 2), jnp.float32)
    return pl.pallas_call(
        products_kernel,
        out_shape=(part, part, jax.ShapeDtypeStruct((rows, 2 * n), jnp.bfloat16)),
        in_specs=[SCALAR, WHOLE, anywhere()],
        scratch_shapes=[pltpu.VMEM(trailing.shape, jnp.float32), pltpu.SemaphoreType.DMA((8,))],
        compiler_params=pltpu.CompilerParams(vmem_limit_bytes=MOST),
        cost_estimate=pl.CostEstimate(flops=0, bytes_accessed=11_000_000, transcendentals=0),
        name="products",
    )(where, panel_t, trailing)


def update_kernel(second, where_ref, left_ref, mixed, trailing, *refs):
    if second:
        top_ref, _, updated, high_ref, low_ref, result, sent = refs
    else:
        pivot, replaced, updated, reflectors, top_ref, high_ref, low_ref, result, sent = refs
    row = where_ref[1]
    n, half = mixed.shape
    steps, tall = result.shape[0], result.shape[1]
    mine = 1 - (row & 1) if second else row & 1
    columns = pl.ds(pl.multiple_of(mine * half, half), half)

    def going(i):
        return pltpu.make_async_copy(result.at[i], updated.at[pl.ds(i * tall, tall), columns], sent.at[i])

    if not second:
        top_ref[...] = jnp.where(row == 0, jnp.concatenate(halves(replaced[...]), axis=1), left_ref[:n, :])
    high, low = halves(mixed[...])
    high_ref[:n], high_ref[n:] = high, high
    low_ref[:n], low_ref[n:] = low, low

    def rows_of(i):
        left = left_ref[i * tall : (i + 1) * tall, :]
        return jnp.concatenate([top_ref[...], left[n:]], axis=0) if i == 0 else left

    def times(left, high, low):
        return jnp.dot(left, high, preferred_element_type=jnp.float32) + jnp.dot(
            left, low, preferred_element_type=jnp.float32
        )

    for first in range(0, steps, 2):
        @pl.when(row >= 0)
        def _():
            for i in range(first, first + 2):
                change = times(rows_of(i), high_ref[...], low_ref[...])
                result[i] = trailing[i * tall : (i + 1) * tall, columns] - change
                going(i).start()

    if not second:
        width = reflectors.shape[0]
        own = pltpu.roll(pivot[...], (n - where_ref[0] * width) % n, 1)
        a, b = halves(own)
        a, b = jnp.concatenate([a, a], axis=0), jnp.concatenate([b, b], axis=0)
        for i in range(steps):
            reflectors[:, i * tall : (i + 1) * tall] = times(rows_of(i), a, b).T[:width]
    for i in range(steps):
        going(i).wait()


def update_call(second, inputs, outs, specs, mixed, trailing, name, aliases):
    n, half = mixed.shape
    rows, _ = trailing.shape
    steps = 8
    return pl.pallas_call(
        lambda *refs: update_kernel(second, *refs),
        out_shape=outs,
        in_specs=[SCALAR, WHOLE, WHOLE, WHOLE] + specs,
        out_specs=(anywhere(),) + (WHOLE,) * (len(outs) - 1),
        scratch_shapes=[pltpu.VMEM((2 * n, half), jnp.bfloat16)] * 2
        + [pltpu.VMEM((steps, rows // steps, half), jnp.float32)]
        + [pltpu.SemaphoreType.DMA((steps,))],
        input_output_aliases=aliases,
        compiler_params=pltpu.CompilerParams(vmem_limit_bytes=8 << 20),
        cost_estimate=FREE,
        name=name,
    )(*inputs)


def update(where, left, mixed, trailing, pivot, replaced, width):
    n, rows = mixed.shape[0], trailing.shape[0]
    outs = (
        jax.ShapeDtypeStruct(trailing.shape, jnp.float32),
        jax.ShapeDtypeStruct((width, rows), jnp.float32),
        jax.ShapeDtypeStruct((n, 2 * n), jnp.bfloat16),
    )
    inputs = (where, left, mixed, trailing, pivot, replaced)
    return update_call(False, inputs, outs, [WHOLE, WHOLE], mixed, trailing, "update", {})


def update_rest(where, left, top, mixed, trailing, updated):
    outs = (jax.ShapeDtypeStruct(trailing.shape, jnp.float32),)
    inputs = (where, left, mixed, trailing, top, updated)
    return update_call(True, inputs, outs, [WHOLE, anywhere()], mixed, trailing, "update_rest", {5: 0})[0]


def mix(mine, theirs, lead, weight, inv):
    def kernel(mine, theirs, lead, weight, inv, mixed):
        rest = lead[...] - dot(weight[...], mine[...] + theirs[...], (1, 0))
        mixed[...] = dot(inv[...], rest, (1, 0))

    return pl.pallas_call(
        kernel,
        out_shape=jax.ShapeDtypeStruct(mine.shape, jnp.float32),
        in_specs=[WHOLE] * 5,
        compiler_params=pltpu.CompilerParams(vmem_limit_bytes=3 << 20),
        cost_estimate=FREE,
        name="mix",
    )(mine, theirs, lead, weight, inv)


def after(x, *others):
    return lax.optimization_barrier((x, *others))[0]


def per_device(panel_block, trailing):
    own = panel_block.T
    col, row = lax.axis_index("col"), lax.axis_index("row")
    where = jnp.stack([col, row]).astype(jnp.int32)
    held = {0: own}
    for bit in reversed(bits_of("col")):
        if bit == 1:
            far = max(held)
            own, held[1] = lax.optimization_barrier((own, swap(own, "col", 1)))
            held[0], held[far] = lax.optimization_barrier((nearby(own), held[far]))
        held.update({m | bit: swap(piece, "col", bit) for m, piece in list(held.items()) if m | bit not in held})
    n = own.shape[0] * len(held)
    bits = bits_of("row")
    odd, half = row & bits[0] != 0, trailing.shape[1] // 2

    lead, _ = lax.optimization_barrier((trailing[:n], held[1]))
    keep, give = lax.optimization_barrier(
        (lead[:, :half], jnp.where(odd, lead[:, :half], lead[:, half:]))
    )
    lead = jnp.where(odd, swap(give, "row", bits[0]), keep)
    lead_got = swap(lead, "row", bits[-1])
    panel_t, mine = gram(where, held)
    keep, give, left = products_of(where, panel_t, trailing)
    got = swap(give, "row", bits[0])
    for bit in bits[1:-1]:
        mine = mine + lax.optimization_barrier((swap(mine, "row", bit), keep))[0]
    lead_got, mine = lax.optimization_barrier((lead_got, mine))
    lead = jnp.where(row & bits[-1] != 0, lead_got, lead)
    mine = mine + swap(mine, "row", bits[-1])
    sums, lead, _ = lax.optimization_barrier((keep + got, lead, mine))
    for bit in reversed(bits[1:-1]):
        lead = jnp.where(row & bit != 0, swap(lead, "row", bit), lead)
    mine = mine + swap(mine, "row", bits[0])
    for bit in bits[1:-1]:
        sums = sums + swap(sums, "row", bit)
    theirs = swap(mine, "col", 1)
    last = swap(sums, "row", bits[-1])
    theirs, sums = lax.optimization_barrier((theirs, sums))
    panel_factor, weight, inv, pivot, replaced, kept = factor(col.astype(jnp.int32).reshape(1) & 1, mine, theirs, trailing)
    mixed = mix(sums, last, lead, weight, inv)
    other = swap(mixed, "row", bits[0])
    updated, reflectors, top = update(where, left, mixed, kept, pivot, replaced, own.shape[0])
    updated = update_rest(where, left, top, other, kept, updated)
    return updated, reflectors.T, panel_factor


def solution(mesh):
    in_specs = (P("row", "col"), P("row", "col"))
    out_specs = (P("row", "col"), P("row", "col"), P())
    return jax.shard_map(per_device, mesh=mesh, in_specs=in_specs, out_specs=out_specs, check_vma=False)
```

```python
import jax
import jax.numpy as jnp
from jax import lax
from jax.experimental import pallas as pl
from jax.experimental.pallas import tpu as pltpu
from jax.sharding import PartitionSpec as P

SUB = 16
GROUP = 2
LAG = 2
HIGHEST, HIGH = lax.Precision.HIGHEST, lax.Precision.HIGH
MOST = 60 << 20
MOST = 50 << 20
PIECES = 1
FREE = pl.CostEstimate(flops=1, bytes_accessed=1, transcendentals=0)
SCALAR = pl.BlockSpec(memory_space=pltpu.SMEM)
WHOLE = pl.BlockSpec(memory_space=pltpu.VMEM)


def dot(a, b, over, precision=HIGHEST):
    return lax.dot_general(
        a, b, (((over[0],), (over[1],)), ((), ())), precision=precision, preferred_element_type=jnp.float32
    )


def interleave(streams):
    steps = [((i + 0.5) / len(stream), k, step) for k, stream in enumerate(streams) for i, step in enumerate(stream)]
    for _, _, step in sorted(steps, key=lambda item: item[:2]):
        step()


def factor_kernel(
    even_ref, mine_ref, theirs_ref, panel_factor_ref, inv_ref, pivot_ref, replaced_ref, g, d, lower, upper, lead_ref, weight_ref
):
    n = mine_ref.shape[0]
    slabs = n // SUB
    sub = lax.broadcasted_iota(jnp.int32, (SUB, n), 0)
    lane = lax.broadcasted_iota(jnp.int32, (SUB, n), 1)
    one = jnp.float32(1.0)
    state = {}

    def rows(s):
        return pl.ds(s * SUB, SUB)

    def spread(block, j):
        return jnp.broadcast_to(block[j : j + 1, :], block.shape)

    def columns(block, s):
        return [jnp.broadcast_to(block[:, k : k + 1], block.shape) for k in range(s * SUB, (s + 1) * SUB)]

    def within(first, last):
        return (lane >= first * SUB) & (lane < last * SUB)

    def group(s):
        first = s // GROUP * GROUP
        return range(first, first + GROUP)

    def reduce_steps(name, s, ref):
        me = state[name, s] = {}
        split = name == "g"

        def begin():
            block = ref[rows(s), :]
            unit = jnp.where(sub + s * SUB == lane, one, 0.0)
            me["cols"] = columns(block, s)
            if split:
                me["arrays"] = [block, jnp.where(lane < s * SUB, block, unit)]
                me["at"] = list(me["arrays"])
            else:
                me["arrays"] = [jnp.where(within(s, s + 1), unit, block)]
                me["upper"] = unit

        def step(j):
            here = sub == j
            cols = me["cols"]
            inv = 1.0 / spread(cols[j], j)
            me["inv"] = inv if j == 0 else jnp.where(here, inv, me["inv"])
            if j and split:
                me["at"] = [jnp.where(here, a, b) for a, b in zip(me["arrays"], me["at"])]
            mult = jnp.where(here, 0.0, cols[j]) * inv
            for c in range(j + 1, SUB):
                cols[c] = cols[c] - mult * spread(cols[c], j)
            me["arrays"] = [a - mult * spread(a, j) for a in me["arrays"]]
            if j and not split:
                me["upper"] = me["upper"] - jnp.where(sub < j, mult, 0.0) * spread(me["upper"], j)

        def end():
            scaled = [a * me["inv"] for a in me["arrays"]]
            whole = jnp.where(lane < (s + 1) * SUB, scaled[1], scaled[0]) if split else scaled[0]
            me["rows"] = [spread(whole, j) for j in range(SUB)]
            ref[rows(s), :] = whole
            if not split:
                full = me["upper"] * me["inv"]
                me["upper_rows"] = [spread(full, j) for j in range(SUB)]
                upper[rows(s), :] = full

        return [begin] + [lambda j=j: step(j) for j in range(SUB)] + [end]

    def eliminate(name, s, t, ref):
        def run():
            block = ref[rows(t), :]
            cols = columns(block, s)
            block = jnp.where(within(s, s + 1), 0.0, block)
            for col, row in zip(cols, state[name, s]["rows"]):
                block = block - col * row
            ref[rows(t), :] = block
            if name == "d" and t < s:
                block = upper[rows(t), :]
                for col, row in zip(cols, state[name, s]["upper_rows"]):
                    block = block - col * row
                upper[rows(t), :] = block

        return run

    def times(a, b):
        return jnp.dot(a, b, precision=lax.Precision.HIGHEST, preferred_element_type=jnp.float32)

    def others(name, s, ref):
        first, last = group(s)[0], group(s)[-1] + 1

        def run():
            whole = ref[...]
            mask = within(first, last)
            if name == "g":
                targets = list(range(last, slabs))
                left = jnp.concatenate([jnp.where(mask, whole[t * SUB : (t + 1) * SUB], 0.0) for t in targets], axis=0)
                change = times(left, whole)
            else:
                targets = list(range(slabs))
                left = jnp.concatenate(
                    [
                        jnp.where(mask, lower[rows(t), :] if t in group(s) else whole[t * SUB : (t + 1) * SUB], 0.0)
                        for t in targets
                    ],
                    axis=0,
                )
                change = times(left, whole)
                below = times(left[first * SUB :], upper[...])
                for i, t in enumerate(range(first, slabs)):
                    part = below[i * SUB : (i + 1) * SUB]
                    lower[rows(t), :] = jnp.where(mask, part, jnp.where(lane < first * SUB, lower[rows(t), :], 0.0))
            for i, t in enumerate(targets):
                if t not in group(s):
                    block = jnp.where(mask, 0.0, whole[t * SUB : (t + 1) * SUB])
                    ref[rows(t), :] = block - change[i * SUB : (i + 1) * SUB]

        return run

    started = set()

    def start_group(s):
        for t in group(s):
            lower[rows(t), :] = jnp.where(lane < s * SUB, lower[rows(t), :], d[rows(t), :]) if s else d[rows(t), :]
            started.add(t)

    def cholesky_out(s):
        me = state["g", s]

        def first():
            scale = jnp.sqrt(me["inv"])
            x_at, y_at = me["at"]
            me["r"] = jnp.where(lane >= sub + s * SUB, x_at * scale, 0.0)
            me["r_inv_t"] = y_at * scale
            diagonal = jnp.sum(lead_ref[rows(s), :] * me["r_inv_t"], axis=1, keepdims=True)
            me["sign"] = jnp.broadcast_to(jnp.where(diagonal >= 0, -one, one), (SUB, n))

        def second():
            signed = me["sign"] * me["r"]
            panel_factor_ref[rows(s), :] = signed
            weight_ref[rows(s), :] = me["sign"] * me["r_inv_t"]
            replaced_ref[rows(s), :] = lead_ref[rows(s), :] - signed
            d[rows(s), :] = d[rows(s), :] - signed
            if s in started:
                lower[rows(s), :] = lower[rows(s), :] - signed

        return [first, second]

    even = even_ref[0] == 0
    g[...] = jnp.where(even, mine_ref[...], theirs_ref[...])
    lead_ref[...] = jnp.where(even, theirs_ref[...], mine_ref[...])
    d[...] = lead_ref[...]
    lower[...] = jnp.zeros((n, n), jnp.float32)
    upper[...] = jnp.zeros((n, n), jnp.float32)
    for k in range(slabs + LAG):
        streams, after = [], []
        if 0 <= k - 1 < slabs:
            streams.append(cholesky_out(k - 1))
        for name, s, ref in (("g", k, g), ("d", k - LAG, d)):
            if not 0 <= s < slabs:
                continue
            if name == "d" and s % GROUP == 0:
                start_group(s)
            if s % GROUP:
                streams.append([eliminate(name, s - 1, t, ref) for t in group(s) if t not in (s - 1, s)])
            chain = reduce_steps(name, s, ref)
            if (s + 1) % GROUP:
                chain.append(eliminate(name, s, s + 1, ref))
            else:
                chain += [eliminate(name, s, t, ref) for t in group(s) if t != s]
                if name == "d" or s + 1 < slabs:
                    after.append(others(name, s, ref))
            streams.append(chain)
        interleave([s for s in streams if s])
        for step in after:
            step()
    inv_ref[:, :n] = d[...]
    inv_ref[:, n:] = -times(d[...], weight_ref[...])
    pivot_ref[...] = times(d[...], lower[...])


def fetching_factor_kernel(odd, mine, theirs, trailing, *refs):
    *outs, held = refs[:5]
    *scratch, got = refs[5:]
    copy = pltpu.make_async_copy(trailing, held, got.at[0])
    copy.start()

    @pl.when(odd[0] >= 0)
    def _():
        factor_kernel(odd, mine, theirs, *outs, *scratch)

    copy.wait()


def factor(odd, mine, theirs, trailing):
    n = mine.shape[0]
    out = jax.ShapeDtypeStruct((n, n), jnp.float32)
    return pl.pallas_call(
        fetching_factor_kernel,
        out_shape=(
            out,
            jax.ShapeDtypeStruct((n, 2 * n), jnp.float32),
            out,
            out,
            jax.ShapeDtypeStruct(trailing.shape, jnp.float32),
        ),
        in_specs=[SCALAR, WHOLE, WHOLE, anywhere()],
        scratch_shapes=[pltpu.VMEM((n, n), jnp.float32)] * 6 + [pltpu.SemaphoreType.DMA((1,))],
        compiler_params=pltpu.CompilerParams(vmem_limit_bytes=47 << 20),
        cost_estimate=pl.CostEstimate(flops=0, bytes_accessed=22_000_000, transcendentals=0),
        name="factor",
    )(odd, mine, theirs, trailing)


def swap(x, axis, mask):
    return lax.ppermute(x, axis, [(i, i ^ mask) for i in range(lax.axis_size(axis))])


def bits_of(axis):
    return [1 << b for b in range(lax.axis_size(axis).bit_length() - 1)]


def halves(x):
    high = x.astype(jnp.bfloat16)
    return high, (x - high.astype(jnp.float32)).astype(jnp.bfloat16)


def anywhere():
    return pl.BlockSpec(memory_space=pl.ANY)


def fetch(trailing, held, got, steps=8):
    tall = trailing.shape[0] // steps
    copies = [
        pltpu.make_async_copy(trailing.at[pl.ds(i * tall, tall)], held.at[pl.ds(i * tall, tall)], got.at[i])
        for i in range(steps)
    ]
    for copy in copies:
        copy.start()
    return copies


def product(pieces, held, copies):
    left = jnp.concatenate([piece[...] for piece in pieces], axis=0)
    high, low = halves(left)
    both = jnp.concatenate([high, low], axis=0)
    m, tall = left.shape[0], held.shape[0] // len(copies)
    sums = jnp.zeros((m, held.shape[1]), jnp.float32)
    for i, copy in enumerate(copies):
        copy.wait()
        right_high, right_low = halves(held[i * tall : (i + 1) * tall, :])
        part = slice(i * tall, (i + 1) * tall)
        one = jnp.dot(both[:, part], right_high, preferred_element_type=jnp.float32)
        two = jnp.dot(high[:, part], right_low, preferred_element_type=jnp.float32)
        sums = sums + (one[:m] + one[m:] + two)
    return sums


def gram_kernel(masks, where_ref, *refs):
    pieces, panel_t, mine = refs[: len(masks)], refs[-2], refs[-1]
    col, row = where_ref[0], where_ref[1]
    width = pieces[0].shape[0]
    n = width * len(masks)
    for mask, piece in zip(masks, pieces):
        panel_t[pl.ds(pl.multiple_of((col ^ mask) * width, width), width), :] = piece[...]

    @pl.when(col & 1 == 0)
    def _():
        whole = panel_t[...]
        high = whole.astype(jnp.bfloat16)
        rest = whole - high.astype(jnp.float32)
        middle = rest.astype(jnp.bfloat16)
        low = (rest - middle.astype(jnp.float32)).astype(jnp.bfloat16)
        parts = lax.dot_general(
            jnp.concatenate([high, middle, low], axis=0),
            jnp.concatenate([high, middle], axis=0),
            (((1,), (1,)), ((), ())),
            preferred_element_type=jnp.float32,
        )
        small = parts[n : 2 * n, n:] + (parts[2 * n :, :n] + parts[2 * n :, :n].T)
        mine[...] = parts[:n, :n] + ((parts[n : 2 * n, :n] + parts[:n, n:]) + small)

    @pl.when(col & 1 == 1)
    def _():
        mine[...] = jnp.where(row == 0, panel_t[:, :n].T, 0.0)


def gram(where, held):
    width, rows = held[0].shape
    n = width * len(held)
    return pl.pallas_call(
        lambda *refs: gram_kernel(tuple(held), *refs),
        out_shape=(jax.ShapeDtypeStruct((n, rows), jnp.float32), jax.ShapeDtypeStruct((n, n), jnp.float32)),
        in_specs=[SCALAR] + [WHOLE] * len(held),
        compiler_params=pltpu.CompilerParams(vmem_limit_bytes=8 << 20),
        cost_estimate=FREE,
        name="gram",
    )(where, *held.values())


def copy_kernel(x, out):
    out[...] = x[...]


def nearby(x):
    return pl.pallas_call(
        copy_kernel,
        out_shape=jax.ShapeDtypeStruct(x.shape, x.dtype),
        in_specs=[WHOLE],
        compiler_params=pltpu.CompilerParams(vmem_limit_bytes=1 << 20),
        cost_estimate=FREE,
        name="nearby",
    )(x)


def products_kernel(where_ref, panel_t, trailing, keep, give, left, held, got):
    copies = fetch(trailing, held, got)
    n, rows = panel_t.shape

    @pl.when(where_ref[1] >= 0)
    def _():
        for i in range(0, rows, n):
            left[i : i + n, :n], left[i : i + n, n:] = halves(panel_t[:, i : i + n].T)
        sums = product([panel_t], held, copies)
        half = sums.shape[1] // 2
        first = where_ref[1] & 1 == 0
        keep[...] = jnp.where(first, sums[:, :half], sums[:, half:])
        give[...] = jnp.where(first, sums[:, half:], sums[:, :half])


def products_of(where, panel_t, trailing):
    (n, rows), cols = panel_t.shape, trailing.shape[1]
    part = jax.ShapeDtypeStruct((n, cols // 2), jnp.float32)
    return pl.pallas_call(
        products_kernel,
        out_shape=(part, part, jax.ShapeDtypeStruct((rows, 2 * n), jnp.bfloat16)),
        in_specs=[SCALAR, WHOLE, anywhere()],
        scratch_shapes=[pltpu.VMEM(trailing.shape, jnp.float32), pltpu.SemaphoreType.DMA((8,))],
        compiler_params=pltpu.CompilerParams(vmem_limit_bytes=MOST),
        cost_estimate=pl.CostEstimate(flops=0, bytes_accessed=11_000_000, transcendentals=0),
        name="products",
    )(where, panel_t, trailing)


def update_kernel(pieces, second, where_ref, left_ref, trailing, *refs):
    mixed, refs = refs[: len(pieces)], refs[len(pieces) :]
    if second:
        top_ref, _, updated, high_ref, low_ref, result, sent = refs
    else:
        pivot, replaced, updated, reflectors, top_ref, high_ref, low_ref, result, sent = refs
    row = where_ref[1]
    n, width = mixed[0].shape
    steps, tall = result.shape[0], result.shape[1]
    mine = 1 - (row & 1) if second else row & 1
    first_piece = pl.multiple_of(mine * (PIECES * width) + pieces[0] * width, width)
    columns = pl.ds(first_piece, len(pieces) * width)

    def going(i):
        return pltpu.make_async_copy(result.at[i], updated.at[pl.ds(i * tall, tall), columns], sent.at[i])

    if not second:
        top_ref[...] = jnp.where(row == 0, jnp.concatenate(halves(replaced[...]), axis=1), left_ref[:n, :])
    high, low = halves(jnp.concatenate([piece[...] for piece in mixed], axis=1))
    high_ref[:n], high_ref[n:] = high, high
    low_ref[:n], low_ref[n:] = low, low

    def rows_of(i):
        left = left_ref[i * tall : (i + 1) * tall, :]
        return jnp.concatenate([top_ref[...], left[n:]], axis=0) if i == 0 else left

    def times(left, high, low):
        return jnp.dot(left, high, preferred_element_type=jnp.float32) + jnp.dot(
            left, low, preferred_element_type=jnp.float32
        )

    for first in range(0, steps, 2):
        @pl.when(row >= 0)
        def _():
            for i in range(first, first + 2):
                change = times(rows_of(i), high_ref[...], low_ref[...])
                result[i] = trailing[i * tall : (i + 1) * tall, columns] - change
                going(i).start()

    if not second:
        width = reflectors.shape[0]
        own = pltpu.roll(pivot[...], (n - where_ref[0] * width) % n, 1)
        a, b = halves(own)
        a, b = jnp.concatenate([a, a], axis=0), jnp.concatenate([b, b], axis=0)
        for i in range(steps):
            reflectors[:, i * tall : (i + 1) * tall] = times(rows_of(i), a, b).T[:width]
    for i in range(steps):
        going(i).wait()


def update_call(pieces, second, where, left, trailing, mixed, inputs, outs, specs, name, aliases):
    n, width = mixed[0].shape
    width *= len(pieces)
    rows, steps = trailing.shape[0], 8
    return pl.pallas_call(
        lambda *refs: update_kernel(pieces, second, *refs),
        out_shape=outs,
        in_specs=[SCALAR, WHOLE, WHOLE] + [WHOLE] * len(pieces) + specs,
        out_specs=(anywhere(),) + (WHOLE,) * (len(outs) - 1),
        scratch_shapes=[pltpu.VMEM((2 * n, width), jnp.bfloat16)] * 2
        + [pltpu.VMEM((steps, rows // steps, width), jnp.float32)]
        + [pltpu.SemaphoreType.DMA((steps,))],
        input_output_aliases=aliases,
        compiler_params=pltpu.CompilerParams(vmem_limit_bytes=8 << 20),
        cost_estimate=FREE,
        name=name,
    )(where, left, trailing, *mixed, *inputs)


def update(where, left, mixed, trailing, pivot, replaced, width):
    n, rows = mixed[0].shape[0], trailing.shape[0]
    outs = (
        jax.ShapeDtypeStruct(trailing.shape, jnp.float32),
        jax.ShapeDtypeStruct((width, rows), jnp.float32),
        jax.ShapeDtypeStruct((n, 2 * n), jnp.bfloat16),
    )
    pieces = tuple(range(PIECES))
    return update_call(
        pieces, False, where, left, trailing, mixed, (pivot, replaced), outs, [WHOLE, WHOLE], "update", {}
    )


def update_rest(piece, where, left, top, mixed, trailing, updated):
    outs = (jax.ShapeDtypeStruct(trailing.shape, jnp.float32),)
    inputs = (top, updated)
    return update_call(
        (piece,), True, where, left, trailing, (mixed,), inputs, outs, [WHOLE, anywhere()], "update_rest", {5: 0}
    )[0]


def mix(mine, theirs, lead, inv):
    def kernel(mine, theirs, lead, inv, *outs):
        right = jnp.concatenate([lead[...], mine[...] + theirs[...]], axis=0)
        mixed = dot(inv[...], right, (1, 0))
        width = outs[0].shape[1]
        for i, out in enumerate(outs):
            out[...] = mixed[:, i * width : (i + 1) * width]

    n, half = mine.shape
    return pl.pallas_call(
        kernel,
        out_shape=(jax.ShapeDtypeStruct((n, half // PIECES), jnp.float32),) * PIECES,
        in_specs=[WHOLE] * 4,
        compiler_params=pltpu.CompilerParams(vmem_limit_bytes=3 << 20),
        cost_estimate=FREE,
        name="mix",
    )(mine, theirs, lead, inv)


def after(x, *others):
    return lax.optimization_barrier((x, *others))[0]


def per_device(panel_block, trailing):
    own = panel_block.T
    col, row = lax.axis_index("col"), lax.axis_index("row")
    where = jnp.stack([col, row]).astype(jnp.int32)
    held = {0: own}
    for bit in reversed(bits_of("col")):
        if bit == 1:
            far = max(held)
            own, held[1] = lax.optimization_barrier((own, swap(own, "col", 1)))
            held[0], held[far] = lax.optimization_barrier((nearby(own), held[far]))
        held.update({m | bit: swap(piece, "col", bit) for m, piece in list(held.items()) if m | bit not in held})
    n = own.shape[0] * len(held)
    bits = bits_of("row")
    odd, half = row & bits[0] != 0, trailing.shape[1] // 2

    lead, _ = lax.optimization_barrier((trailing[:n], held[1]))
    keep, give = lax.optimization_barrier(
        (lead[:, :half], jnp.where(odd, lead[:, :half], lead[:, half:]))
    )
    lead = jnp.where(odd, swap(give, "row", bits[0]), keep)
    for bit in bits[1:-1]:
        lead = jnp.where(row & bit != 0, swap(lead, "row", bit), lead)
    panel_t, mine = gram(where, held)
    keep, give, left = products_of(where, panel_t, trailing)
    got = swap(give, "row", bits[0])
    for bit in bits[1:-1]:
        mine = mine + lax.optimization_barrier((swap(mine, "row", bit), keep))[0]
    lead, mine = lax.optimization_barrier((lead, mine))
    got_z = swap(mine, "row", bits[-1])
    mine = mine + got_z
    sums, lead, mine = lax.optimization_barrier((keep + got, lead, mine))
    lead_got = swap(lead, "row", bits[-1])
    mine = mine + swap(mine, "row", bits[0])
    for bit in bits[1:-1]:
        sums = sums + swap(sums, "row", bit)
    theirs = swap(mine, "col", 1)
    last = swap(sums, "row", bits[-1])
    theirs, sums = lax.optimization_barrier((theirs, sums))
    lead = jnp.where(row & bits[-1] != 0, lead_got, lead)
    odd_col = col.astype(jnp.int32).reshape(1) & 1
    panel_factor, inv, pivot, replaced, kept = factor(odd_col, mine, theirs, trailing)
    mixed = mix(sums, last, lead, inv)
    others = [swap(piece, "row", bits[0]) for piece in mixed]
    updated, reflectors, top = update(where, left, mixed, kept, pivot, replaced, own.shape[0])
    for i, other in enumerate(others):
        updated = update_rest(i, where, left, top, other, kept, updated)
    return updated, reflectors.T, panel_factor


def solution(mesh):
    in_specs = (P("row", "col"), P("row", "col"))
    out_specs = (P("row", "col"), P("row", "col"), P())
    return jax.shard_map(per_device, mesh=mesh, in_specs=in_specs, out_specs=out_specs, check_vma=False)
```

```python
import jax
import jax.numpy as jnp
from jax import lax
from jax.experimental import pallas as pl
from jax.experimental.pallas import tpu as pltpu
from jax.sharding import PartitionSpec as P

SUB = 16
GROUP = 2
LAG = 1
HIGHEST, HIGH = lax.Precision.HIGHEST, lax.Precision.HIGH
MOST = 60 << 20
MOST = 50 << 20
PIECES = 1
FREE = pl.CostEstimate(flops=1, bytes_accessed=1, transcendentals=0)
SCALAR = pl.BlockSpec(memory_space=pltpu.SMEM)
WHOLE = pl.BlockSpec(memory_space=pltpu.VMEM)


def dot(a, b, over, precision=HIGHEST):
    return lax.dot_general(
        a, b, (((over[0],), (over[1],)), ((), ())), precision=precision, preferred_element_type=jnp.float32
    )


def interleave(streams):
    steps = [((i + 0.5) / len(stream), k, step) for k, stream in enumerate(streams) for i, step in enumerate(stream)]
    for _, _, step in sorted(steps, key=lambda item: item[:2]):
        step()


def factor_kernel(
    even_ref, mine_ref, theirs_ref, panel_factor_ref, inv_ref, pivot_ref, replaced_ref, g, d, lower, upper, lead_ref, weight_ref
):
    n = mine_ref.shape[0]
    slabs = n // SUB
    sub = lax.broadcasted_iota(jnp.int32, (SUB, n), 0)
    lane = lax.broadcasted_iota(jnp.int32, (SUB, n), 1)
    one = jnp.float32(1.0)
    state = {}

    def rows(s):
        return pl.ds(s * SUB, SUB)

    def spread(block, j):
        return jnp.broadcast_to(block[j : j + 1, :], block.shape)

    def columns(block, s):
        return [jnp.broadcast_to(block[:, k : k + 1], block.shape) for k in range(s * SUB, (s + 1) * SUB)]

    def within(first, last):
        return (lane >= first * SUB) & (lane < last * SUB)

    def group(s):
        first = s // GROUP * GROUP
        return range(first, first + GROUP)

    def reduce_steps(name, s, ref):
        me = state[name, s] = {}
        split = name == "g"

        def begin():
            block = ref[rows(s), :]
            unit = jnp.where(sub + s * SUB == lane, one, 0.0)
            me["cols"] = columns(block, s)
            if split:
                me["arrays"] = [block, jnp.where(lane < s * SUB, block, unit)]
                me["at"] = list(me["arrays"])
            else:
                me["arrays"] = [jnp.where(within(s, s + 1), unit, block)]
                me["upper"] = unit

        def step(j):
            here = sub == j
            cols = me["cols"]
            inv = 1.0 / spread(cols[j], j)
            me["inv"] = inv if j == 0 else jnp.where(here, inv, me["inv"])
            if j and split:
                me["at"] = [jnp.where(here, a, b) for a, b in zip(me["arrays"], me["at"])]
            mult = jnp.where(here, 0.0, cols[j]) * inv
            for c in range(j + 1, SUB):
                cols[c] = cols[c] - mult * spread(cols[c], j)
            me["arrays"] = [a - mult * spread(a, j) for a in me["arrays"]]
            if j and not split:
                me["upper"] = me["upper"] - jnp.where(sub < j, mult, 0.0) * spread(me["upper"], j)

        def end():
            scaled = [a * me["inv"] for a in me["arrays"]]
            whole = jnp.where(lane < (s + 1) * SUB, scaled[1], scaled[0]) if split else scaled[0]
            me["rows"] = [spread(whole, j) for j in range(SUB)]
            ref[rows(s), :] = whole
            if not split:
                full = me["upper"] * me["inv"]
                me["upper_rows"] = [spread(full, j) for j in range(SUB)]
                upper[rows(s), :] = full

        return [begin] + [lambda j=j: step(j) for j in range(SUB)] + [end]

    def eliminate(name, s, t, ref):
        def run():
            block = ref[rows(t), :]
            cols = columns(block, s)
            block = jnp.where(within(s, s + 1), 0.0, block)
            for col, row in zip(cols, state[name, s]["rows"]):
                block = block - col * row
            ref[rows(t), :] = block
            if name == "d" and t < s:
                block = upper[rows(t), :]
                for col, row in zip(cols, state[name, s]["upper_rows"]):
                    block = block - col * row
                upper[rows(t), :] = block

        return run

    def times(a, b):
        return jnp.dot(a, b, precision=lax.Precision.HIGHEST, preferred_element_type=jnp.float32)

    def others(name, s, ref):
        first, last = group(s)[0], group(s)[-1] + 1

        def run():
            whole = ref[...]
            mask = within(first, last)
            if name == "g":
                targets = list(range(last, slabs))
                left = jnp.concatenate([jnp.where(mask, whole[t * SUB : (t + 1) * SUB], 0.0) for t in targets], axis=0)
                change = times(left, whole)
            else:
                targets = [*range(last, slabs), *range(first, last), *range(first)]
                left = jnp.concatenate(
                    [
                        jnp.where(mask, lower[rows(t), :] if t in group(s) else whole[t * SUB : (t + 1) * SUB], 0.0)
                        for t in targets
                    ],
                    axis=0,
                )
                change = times(left, whole)
                below = times(left[: (slabs - first) * SUB], upper[...])
                for i, t in enumerate(targets[: slabs - first]):
                    part = below[i * SUB : (i + 1) * SUB]
                    lower[rows(t), :] = jnp.where(mask, part, jnp.where(lane < first * SUB, lower[rows(t), :], 0.0))
            for i, t in enumerate(targets):
                if t not in group(s):
                    block = jnp.where(mask, 0.0, whole[t * SUB : (t + 1) * SUB])
                    ref[rows(t), :] = block - change[i * SUB : (i + 1) * SUB]

        return run

    started = set()

    def start_group(s):
        for t in group(s):
            lower[rows(t), :] = jnp.where(lane < s * SUB, lower[rows(t), :], d[rows(t), :]) if s else d[rows(t), :]
            started.add(t)

    def cholesky_out(s):
        me = state["g", s]

        def first():
            scale = jnp.sqrt(me["inv"])
            x_at, y_at = me["at"]
            me["r"] = jnp.where(lane >= sub + s * SUB, x_at * scale, 0.0)
            me["r_inv_t"] = y_at * scale
            diagonal = jnp.sum(lead_ref[rows(s), :] * me["r_inv_t"], axis=1, keepdims=True)
            me["sign"] = jnp.broadcast_to(jnp.where(diagonal >= 0, -one, one), (SUB, n))

        def second():
            signed = me["sign"] * me["r"]
            panel_factor_ref[rows(s), :] = signed
            weight_ref[rows(s), :] = me["sign"] * me["r_inv_t"]
            replaced_ref[rows(s), :] = lead_ref[rows(s), :] - signed
            d[rows(s), :] = d[rows(s), :] - signed
            if s in started:
                lower[rows(s), :] = lower[rows(s), :] - signed

        return [first, second]

    even = even_ref[0] == 0
    g[...] = jnp.where(even, mine_ref[...], theirs_ref[...])
    lead_ref[...] = jnp.where(even, theirs_ref[...], mine_ref[...])
    d[...] = lead_ref[...]
    lower[...] = jnp.zeros((n, n), jnp.float32)
    upper[...] = jnp.zeros((n, n), jnp.float32)
    for k in range(slabs + LAG):
        streams, after = [], []
        if 0 <= k - 1 < slabs:
            for step in cholesky_out(k - 1):
                step()
        for name, s, ref in (("d", k - LAG, d), ("g", k, g)):
            if not 0 <= s < slabs:
                continue
            if name == "d" and s % GROUP == 0:
                start_group(s)
            if s % GROUP:
                streams.append([eliminate(name, s - 1, t, ref) for t in group(s) if t not in (s - 1, s)])
            chain = reduce_steps(name, s, ref)
            if (s + 1) % GROUP:
                chain.append(eliminate(name, s, s + 1, ref))
            else:
                chain += [eliminate(name, s, t, ref) for t in group(s) if t != s]
                if name == "d" or s + 1 < slabs:
                    after.append(others(name, s, ref))
            streams.append(chain)
        interleave([s for s in streams if s])
        for step in after:
            step()
    inv_ref[:, :n] = d[...]
    last_two = times(d[...], jnp.concatenate([weight_ref[...], lower[...]], axis=1))
    inv_ref[:, n:] = -last_two[:, :n]
    pivot_ref[...] = last_two[:, n:]


def fetching_factor_kernel(odd, mine, theirs, trailing, *refs):
    *outs, held = refs[:5]
    *scratch, got = refs[5:]
    copy = pltpu.make_async_copy(trailing, held, got.at[0])
    copy.start()

    @pl.when(odd[0] >= 0)
    def _():
        factor_kernel(odd, mine, theirs, *outs, *scratch)

    copy.wait()


def factor(odd, mine, theirs, trailing):
    n = mine.shape[0]
    out = jax.ShapeDtypeStruct((n, n), jnp.float32)
    return pl.pallas_call(
        fetching_factor_kernel,
        out_shape=(
            out,
            jax.ShapeDtypeStruct((n, 2 * n), jnp.float32),
            out,
            out,
            jax.ShapeDtypeStruct(trailing.shape, jnp.float32),
        ),
        in_specs=[SCALAR, WHOLE, WHOLE, anywhere()],
        scratch_shapes=[pltpu.VMEM((n, n), jnp.float32)] * 6 + [pltpu.SemaphoreType.DMA((1,))],
        compiler_params=pltpu.CompilerParams(vmem_limit_bytes=47 << 20),
        cost_estimate=pl.CostEstimate(flops=0, bytes_accessed=22_000_000, transcendentals=0),
        name="factor",
    )(odd, mine, theirs, trailing)


def swap(x, axis, mask):
    return lax.ppermute(x, axis, [(i, i ^ mask) for i in range(lax.axis_size(axis))])


def bits_of(axis):
    return [1 << b for b in range(lax.axis_size(axis).bit_length() - 1)]


def halves(x):
    high = x.astype(jnp.bfloat16)
    return high, (x - high.astype(jnp.float32)).astype(jnp.bfloat16)


def anywhere():
    return pl.BlockSpec(memory_space=pl.ANY)


def fetch(trailing, held, got, steps=8):
    tall = trailing.shape[0] // steps
    copies = [
        pltpu.make_async_copy(trailing.at[pl.ds(i * tall, tall)], held.at[pl.ds(i * tall, tall)], got.at[i])
        for i in range(steps)
    ]
    for copy in copies:
        copy.start()
    return copies


def product(pieces, held, copies):
    left = jnp.concatenate([piece[...] for piece in pieces], axis=0)
    high, low = halves(left)
    both = jnp.concatenate([high, low], axis=0)
    m, tall = left.shape[0], held.shape[0] // len(copies)
    sums = jnp.zeros((m, held.shape[1]), jnp.float32)
    for i, copy in enumerate(copies):
        copy.wait()
        right_high, right_low = halves(held[i * tall : (i + 1) * tall, :])
        part = slice(i * tall, (i + 1) * tall)
        one = jnp.dot(both[:, part], right_high, preferred_element_type=jnp.float32)
        two = jnp.dot(high[:, part], right_low, preferred_element_type=jnp.float32)
        sums = sums + (one[:m] + one[m:] + two)
    return sums


def gram_kernel(masks, where_ref, *refs):
    pieces, panel_t, mine = refs[: len(masks)], refs[-2], refs[-1]
    col, row = where_ref[0], where_ref[1]
    width = pieces[0].shape[0]
    n = width * len(masks)
    for mask, piece in zip(masks, pieces):
        panel_t[pl.ds(pl.multiple_of((col ^ mask) * width, width), width), :] = piece[...]

    @pl.when(col & 1 == 0)
    def _():
        whole = panel_t[...]
        high = whole.astype(jnp.bfloat16)
        rest = whole - high.astype(jnp.float32)
        middle = rest.astype(jnp.bfloat16)
        low = (rest - middle.astype(jnp.float32)).astype(jnp.bfloat16)
        parts = lax.dot_general(
            jnp.concatenate([high, middle, low], axis=0),
            jnp.concatenate([high, middle], axis=0),
            (((1,), (1,)), ((), ())),
            preferred_element_type=jnp.float32,
        )
        small = parts[n : 2 * n, n:] + (parts[2 * n :, :n] + parts[2 * n :, :n].T)
        mine[...] = parts[:n, :n] + ((parts[n : 2 * n, :n] + parts[:n, n:]) + small)

    @pl.when(col & 1 == 1)
    def _():
        mine[...] = jnp.where(row == 0, panel_t[:, :n].T, 0.0)


def gram(where, held):
    width, rows = held[0].shape
    n = width * len(held)
    return pl.pallas_call(
        lambda *refs: gram_kernel(tuple(held), *refs),
        out_shape=(jax.ShapeDtypeStruct((n, rows), jnp.float32), jax.ShapeDtypeStruct((n, n), jnp.float32)),
        in_specs=[SCALAR] + [WHOLE] * len(held),
        compiler_params=pltpu.CompilerParams(vmem_limit_bytes=8 << 20),
        cost_estimate=FREE,
        name="gram",
    )(where, *held.values())


def copy_kernel(x, out):
    out[...] = x[...]


def nearby(x):
    return pl.pallas_call(
        copy_kernel,
        out_shape=jax.ShapeDtypeStruct(x.shape, x.dtype),
        in_specs=[WHOLE],
        compiler_params=pltpu.CompilerParams(vmem_limit_bytes=1 << 20),
        cost_estimate=FREE,
        name="nearby",
    )(x)


def products_kernel(where_ref, panel_t, trailing, keep, give, left, held, got):
    copies = fetch(trailing, held, got)
    n, rows = panel_t.shape

    @pl.when(where_ref[1] >= 0)
    def _():
        for i in range(0, rows, n):
            left[i : i + n, :n], left[i : i + n, n:] = halves(panel_t[:, i : i + n].T)
        sums = product([panel_t], held, copies)
        half = sums.shape[1] // 2
        first = where_ref[1] & 1 == 0
        keep[...] = jnp.where(first, sums[:, :half], sums[:, half:])
        give[...] = jnp.where(first, sums[:, half:], sums[:, :half])


def products_of(where, panel_t, trailing):
    (n, rows), cols = panel_t.shape, trailing.shape[1]
    part = jax.ShapeDtypeStruct((n, cols // 2), jnp.float32)
    return pl.pallas_call(
        products_kernel,
        out_shape=(part, part, jax.ShapeDtypeStruct((rows, 2 * n), jnp.bfloat16)),
        in_specs=[SCALAR, WHOLE, anywhere()],
        scratch_shapes=[pltpu.VMEM(trailing.shape, jnp.float32), pltpu.SemaphoreType.DMA((8,))],
        compiler_params=pltpu.CompilerParams(vmem_limit_bytes=MOST),
        cost_estimate=pl.CostEstimate(flops=0, bytes_accessed=11_000_000, transcendentals=0),
        name="products",
    )(where, panel_t, trailing)


def update_kernel(pieces, second, where_ref, left_ref, trailing, *refs):
    mixed, refs = refs[: len(pieces)], refs[len(pieces) :]
    if second:
        top_ref, _, updated, high_ref, low_ref, result, sent = refs
    else:
        pivot, replaced, updated, reflectors, top_ref, high_ref, low_ref, result, sent = refs
    row = where_ref[1]
    n, width = mixed[0].shape
    steps, tall = result.shape[0], result.shape[1]
    mine = 1 - (row & 1) if second else row & 1
    first_piece = pl.multiple_of(mine * (PIECES * width) + pieces[0] * width, width)
    columns = pl.ds(first_piece, len(pieces) * width)

    def going(i):
        return pltpu.make_async_copy(result.at[i], updated.at[pl.ds(i * tall, tall), columns], sent.at[i])

    if not second:
        top_ref[...] = jnp.where(row == 0, jnp.concatenate(halves(replaced[...]), axis=1), left_ref[:n, :])
    high, low = halves(jnp.concatenate([piece[...] for piece in mixed], axis=1))
    high_ref[:n], high_ref[n:] = high, high
    low_ref[:n], low_ref[n:] = low, low

    def rows_of(i):
        left = left_ref[i * tall : (i + 1) * tall, :]
        return jnp.concatenate([top_ref[...], left[n:]], axis=0) if i == 0 else left

    def times(left, high, low):
        return jnp.dot(left, high, preferred_element_type=jnp.float32) + jnp.dot(
            left, low, preferred_element_type=jnp.float32
        )

    for first in range(0, steps, 2):
        @pl.when(row >= 0)
        def _():
            for i in range(first, first + 2):
                change = times(rows_of(i), high_ref[...], low_ref[...])
                result[i] = trailing[i * tall : (i + 1) * tall, columns] - change
                going(i).start()

    if not second:
        width = reflectors.shape[0]
        own = pltpu.roll(pivot[...], (n - where_ref[0] * width) % n, 1)
        a, b = halves(own)
        a, b = jnp.concatenate([a, a], axis=0), jnp.concatenate([b, b], axis=0)
        for i in range(steps):
            reflectors[:, i * tall : (i + 1) * tall] = times(rows_of(i), a, b).T[:width]
    for i in range(steps):
        going(i).wait()


def update_call(pieces, second, where, left, trailing, mixed, inputs, outs, specs, name, aliases):
    n, width = mixed[0].shape
    width *= len(pieces)
    rows, steps = trailing.shape[0], 8
    return pl.pallas_call(
        lambda *refs: update_kernel(pieces, second, *refs),
        out_shape=outs,
        in_specs=[SCALAR, WHOLE, WHOLE] + [WHOLE] * len(pieces) + specs,
        out_specs=(anywhere(),) + (WHOLE,) * (len(outs) - 1),
        scratch_shapes=[pltpu.VMEM((2 * n, width), jnp.bfloat16)] * 2
        + [pltpu.VMEM((steps, rows // steps, width), jnp.float32)]
        + [pltpu.SemaphoreType.DMA((steps,))],
        input_output_aliases=aliases,
        compiler_params=pltpu.CompilerParams(vmem_limit_bytes=8 << 20),
        cost_estimate=FREE,
        name=name,
    )(where, left, trailing, *mixed, *inputs)


def update(where, left, mixed, trailing, pivot, replaced, width):
    n, rows = mixed[0].shape[0], trailing.shape[0]
    outs = (
        jax.ShapeDtypeStruct(trailing.shape, jnp.float32),
        jax.ShapeDtypeStruct((width, rows), jnp.float32),
        jax.ShapeDtypeStruct((n, 2 * n), jnp.bfloat16),
    )
    pieces = tuple(range(PIECES))
    return update_call(
        pieces, False, where, left, trailing, mixed, (pivot, replaced), outs, [WHOLE, WHOLE], "update", {}
    )


def update_rest(piece, where, left, top, mixed, trailing, updated):
    outs = (jax.ShapeDtypeStruct(trailing.shape, jnp.float32),)
    inputs = (top, updated)
    return update_call(
        (piece,), True, where, left, trailing, (mixed,), inputs, outs, [WHOLE, anywhere()], "update_rest", {5: 0}
    )[0]


def mix(mine, theirs, lead, inv):
    def kernel(mine, theirs, lead, inv, *outs):
        right = jnp.concatenate([lead[...], mine[...] + theirs[...]], axis=0)
        mixed = dot(inv[...], right, (1, 0))
        width = outs[0].shape[1]
        for i, out in enumerate(outs):
            out[...] = mixed[:, i * width : (i + 1) * width]

    n, half = mine.shape
    return pl.pallas_call(
        kernel,
        out_shape=(jax.ShapeDtypeStruct((n, half // PIECES), jnp.float32),) * PIECES,
        in_specs=[WHOLE] * 4,
        compiler_params=pltpu.CompilerParams(vmem_limit_bytes=3 << 20),
        cost_estimate=FREE,
        name="mix",
    )(mine, theirs, lead, inv)


def after(x, *others):
    return lax.optimization_barrier((x, *others))[0]


def per_device(panel_block, trailing):
    own = panel_block.T
    col, row = lax.axis_index("col"), lax.axis_index("row")
    where = jnp.stack([col, row]).astype(jnp.int32)
    held = {0: own}
    for bit in reversed(bits_of("col")):
        if bit == 1:
            far = max(held)
            own, held[1] = lax.optimization_barrier((own, swap(own, "col", 1)))
            held[0], held[far] = lax.optimization_barrier((nearby(own), held[far]))
        held.update({m | bit: swap(piece, "col", bit) for m, piece in list(held.items()) if m | bit not in held})
    n = own.shape[0] * len(held)
    bits = bits_of("row")
    odd, half = row & bits[0] != 0, trailing.shape[1] // 2

    lead, _ = lax.optimization_barrier((trailing[:n], held[1]))
    keep, give = lax.optimization_barrier(
        (lead[:, :half], jnp.where(odd, lead[:, :half], lead[:, half:]))
    )
    lead = jnp.where(odd, swap(give, "row", bits[0]), keep)
    for bit in bits[1:-1]:
        lead = jnp.where(row & bit != 0, swap(lead, "row", bit), lead)
    panel_t, mine = gram(where, held)
    keep, give, left = products_of(where, panel_t, trailing)
    got = swap(give, "row", bits[0])
    for bit in bits[1:-1]:
        mine = mine + lax.optimization_barrier((swap(mine, "row", bit), keep))[0]
    lead, mine = lax.optimization_barrier((lead, mine))
    got_z = swap(mine, "row", bits[-1])
    mine = mine + got_z
    sums, lead, mine = lax.optimization_barrier((keep + got, lead, mine))
    lead_got = swap(lead, "row", bits[-1])
    mine = mine + swap(mine, "row", bits[0])
    for bit in bits[1:-1]:
        sums = sums + swap(sums, "row", bit)
    theirs = swap(mine, "col", 1)
    last = swap(sums, "row", bits[-1])
    theirs, sums = lax.optimization_barrier((theirs, sums))
    lead = jnp.where(row & bits[-1] != 0, lead_got, lead)
    odd_col = col.astype(jnp.int32).reshape(1) & 1
    panel_factor, inv, pivot, replaced, kept = factor(odd_col, mine, theirs, trailing)
    mixed = mix(sums, last, lead, inv)
    others = [swap(piece, "row", bits[0]) for piece in mixed]
    updated, reflectors, top = update(where, left, mixed, kept, pivot, replaced, own.shape[0])
    for i, other in enumerate(others):
        updated = update_rest(i, where, left, top, other, kept, updated)
    return updated, reflectors.T, panel_factor


def solution(mesh):
    in_specs = (P("row", "col"), P("row", "col"))
    out_specs = (P("row", "col"), P("row", "col"), P())
    return jax.shard_map(per_device, mesh=mesh, in_specs=in_specs, out_specs=out_specs, check_vma=False)
```

```python
import jax
import jax.numpy as jnp
from jax import lax
from jax.experimental import pallas as pl
from jax.experimental.pallas import tpu as pltpu
from jax.sharding import PartitionSpec as P

SUB = 16
GROUP = 2
LAG = 1
HIGHEST, HIGH = lax.Precision.HIGHEST, lax.Precision.HIGH
MOST = 60 << 20
MOST = 50 << 20
PIECES = 1
FREE = pl.CostEstimate(flops=1, bytes_accessed=1, transcendentals=0)
SCALAR = pl.BlockSpec(memory_space=pltpu.SMEM)
WHOLE = pl.BlockSpec(memory_space=pltpu.VMEM)


def dot(a, b, over, precision=HIGHEST):
    return lax.dot_general(
        a, b, (((over[0],), (over[1],)), ((), ())), precision=precision, preferred_element_type=jnp.float32
    )


def interleave(streams):
    steps = [((i + 0.5) / len(stream), k, step) for k, stream in enumerate(streams) for i, step in enumerate(stream)]
    for _, _, step in sorted(steps, key=lambda item: item[:2]):
        step()


def factor_kernel(
    even_ref, mine_ref, theirs_ref, panel_factor_ref, inv_ref, pivot_ref, replaced_ref, g, d, lower, upper, lead_ref, weight_ref
):
    n = mine_ref.shape[0]
    slabs = n // SUB
    sub = lax.broadcasted_iota(jnp.int32, (SUB, n), 0)
    lane = lax.broadcasted_iota(jnp.int32, (SUB, n), 1)
    one = jnp.float32(1.0)
    state = {}

    def rows(s):
        return pl.ds(s * SUB, SUB)

    def spread(block, j):
        return jnp.broadcast_to(block[j : j + 1, :], block.shape)

    def columns(block, s):
        return [jnp.broadcast_to(block[:, k : k + 1], block.shape) for k in range(s * SUB, (s + 1) * SUB)]

    def within(first, last):
        return (lane >= first * SUB) & (lane < last * SUB)

    def group(s):
        first = s // GROUP * GROUP
        return range(first, first + GROUP)

    def reduce_steps(name, s, ref):
        me = state[name, s] = {}
        split = name == "g"

        def begin():
            block = ref[rows(s), :]
            unit = jnp.where(sub + s * SUB == lane, one, 0.0)
            me["cols"] = columns(block, s)
            if split:
                me["arrays"] = [block, jnp.where(lane < s * SUB, block, unit)]
                me["at"] = list(me["arrays"])
            else:
                me["arrays"] = [jnp.where(within(s, s + 1), unit, block)]
                me["upper"] = unit

        def step(j):
            here = sub == j
            cols = me["cols"]
            inv = 1.0 / spread(cols[j], j)
            me["inv"] = inv if j == 0 else jnp.where(here, inv, me["inv"])
            if j and split:
                me["at"] = [jnp.where(here, a, b) for a, b in zip(me["arrays"], me["at"])]
            mult = jnp.where(here, 0.0, cols[j]) * inv
            for c in range(j + 1, SUB):
                cols[c] = cols[c] - mult * spread(cols[c], j)
            me["arrays"] = [a - mult * spread(a, j) for a in me["arrays"]]
            if j and not split:
                me["upper"] = me["upper"] - jnp.where(sub < j, mult, 0.0) * spread(me["upper"], j)

        def end():
            scaled = [a * me["inv"] for a in me["arrays"]]
            whole = jnp.where(lane < (s + 1) * SUB, scaled[1], scaled[0]) if split else scaled[0]
            me["rows"] = [spread(whole, j) for j in range(SUB)]
            ref[rows(s), :] = whole
            if not split:
                full = me["upper"] * me["inv"]
                me["upper_rows"] = [spread(full, j) for j in range(SUB)]
                upper[rows(s), :] = full

        return [begin] + [lambda j=j: step(j) for j in range(SUB)] + [end]

    def eliminate(name, s, t, ref):
        def run():
            block = ref[rows(t), :]
            cols = columns(block, s)
            block = jnp.where(within(s, s + 1), 0.0, block)
            for col, row in zip(cols, state[name, s]["rows"]):
                block = block - col * row
            ref[rows(t), :] = block
            if name == "d" and t < s:
                block = upper[rows(t), :]
                for col, row in zip(cols, state[name, s]["upper_rows"]):
                    block = block - col * row
                upper[rows(t), :] = block

        return run

    def times(a, b):
        return jnp.dot(a, b, precision=lax.Precision.HIGHEST, preferred_element_type=jnp.float32)

    def others(name, s, ref):
        first, last = group(s)[0], group(s)[-1] + 1

        def run():
            whole = ref[...]
            mask = within(first, last)
            if name == "g":
                targets = list(range(last, slabs))
                left = jnp.concatenate([jnp.where(mask, whole[t * SUB : (t + 1) * SUB], 0.0) for t in targets], axis=0)
                change = times(left, whole)
            else:
                targets = [*range(last, slabs), *range(first, last), *range(first)]
                left = jnp.concatenate(
                    [
                        jnp.where(mask, lower[rows(t), :] if t in group(s) else whole[t * SUB : (t + 1) * SUB], 0.0)
                        for t in targets
                    ],
                    axis=0,
                )
                change = times(left, whole)
                below = times(left[: (slabs - first) * SUB], upper[...])
                for i, t in enumerate(targets[: slabs - first]):
                    part = below[i * SUB : (i + 1) * SUB]
                    lower[rows(t), :] = jnp.where(mask, part, jnp.where(lane < first * SUB, lower[rows(t), :], 0.0))
            for i, t in enumerate(targets):
                if t not in group(s):
                    block = jnp.where(mask, 0.0, whole[t * SUB : (t + 1) * SUB])
                    ref[rows(t), :] = block - change[i * SUB : (i + 1) * SUB]

        return run

    started = set()

    def start_group(s):
        for t in group(s):
            lower[rows(t), :] = jnp.where(lane < s * SUB, lower[rows(t), :], d[rows(t), :]) if s else d[rows(t), :]
            started.add(t)

    def cholesky_out(s):
        me = state["g", s]

        def first():
            scale = jnp.sqrt(me["inv"])
            x_at, y_at = me["at"]
            me["r"] = jnp.where(lane >= sub + s * SUB, x_at * scale, 0.0)
            me["r_inv_t"] = y_at * scale
            diagonal = jnp.sum(lead_ref[rows(s), :] * me["r_inv_t"], axis=1, keepdims=True)
            me["sign"] = jnp.broadcast_to(jnp.where(diagonal >= 0, -one, one), (SUB, n))

        def second():
            signed = me["sign"] * me["r"]
            panel_factor_ref[rows(s), :] = signed
            weight_ref[rows(s), :] = me["sign"] * me["r_inv_t"]
            replaced_ref[rows(s), :] = lead_ref[rows(s), :] - signed
            d[rows(s), :] = d[rows(s), :] - signed
            if s in started:
                lower[rows(s), :] = lower[rows(s), :] - signed

        return [first, second]

    even = even_ref[0] == 0
    g[...] = jnp.where(even, mine_ref[...], theirs_ref[...])
    lead_ref[...] = jnp.where(even, theirs_ref[...], mine_ref[...])
    d[...] = lead_ref[...]
    lower[...] = jnp.zeros((n, n), jnp.float32)
    upper[...] = jnp.zeros((n, n), jnp.float32)
    for k in range(slabs + LAG):
        streams, after = [], []
        if 0 <= k - 1 < slabs:
            for step in cholesky_out(k - 1):
                step()
        for name, s, ref in (("d", k - LAG, d), ("g", k, g)):
            if not 0 <= s < slabs:
                continue
            if name == "d" and s % GROUP == 0:
                start_group(s)
            if s % GROUP:
                streams.append([eliminate(name, s - 1, t, ref) for t in group(s) if t not in (s - 1, s)])
            chain = reduce_steps(name, s, ref)
            if (s + 1) % GROUP:
                chain.append(eliminate(name, s, s + 1, ref))
            else:
                chain += [eliminate(name, s, t, ref) for t in group(s) if t != s]
                if name == "d" or s + 1 < slabs:
                    after.append(others(name, s, ref))
            streams.append(chain)
        interleave([s for s in streams if s])
        for step in after:
            step()
    inv_ref[:, :n] = d[...]
    last_two = times(d[...], jnp.concatenate([weight_ref[...], lower[...]], axis=1))
    inv_ref[:, n:] = -last_two[:, :n]
    pivot_ref[...] = last_two[:, n:]


def fetching_factor_kernel(odd, mine, theirs, trailing, *refs):
    *outs, held = refs[:5]
    *scratch, got = refs[5:]
    copy = pltpu.make_async_copy(trailing, held, got.at[0])
    copy.start()

    @pl.when(odd[0] >= 0)
    def _():
        factor_kernel(odd, mine, theirs, *outs, *scratch)

    copy.wait()


def factor(odd, mine, theirs, trailing):
    n = mine.shape[0]
    out = jax.ShapeDtypeStruct((n, n), jnp.float32)
    return pl.pallas_call(
        fetching_factor_kernel,
        out_shape=(
            out,
            jax.ShapeDtypeStruct((n, 2 * n), jnp.float32),
            out,
            out,
            jax.ShapeDtypeStruct(trailing.shape, jnp.float32),
        ),
        in_specs=[SCALAR, WHOLE, WHOLE, anywhere()],
        scratch_shapes=[pltpu.VMEM((n, n), jnp.float32)] * 6 + [pltpu.SemaphoreType.DMA((1,))],
        compiler_params=pltpu.CompilerParams(vmem_limit_bytes=47 << 20),
        cost_estimate=pl.CostEstimate(flops=0, bytes_accessed=22_000_000, transcendentals=0),
        name="factor",
    )(odd, mine, theirs, trailing)


def swap(x, axis, mask):
    return lax.ppermute(x, axis, [(i, i ^ mask) for i in range(lax.axis_size(axis))])


def bits_of(axis):
    return [1 << b for b in range(lax.axis_size(axis).bit_length() - 1)]


def halves(x):
    high = x.astype(jnp.bfloat16)
    return high, (x - high.astype(jnp.float32)).astype(jnp.bfloat16)


def anywhere():
    return pl.BlockSpec(memory_space=pl.ANY)


def fetch(trailing, held, got, steps=8):
    tall = trailing.shape[0] // steps
    copies = [
        pltpu.make_async_copy(trailing.at[pl.ds(i * tall, tall)], held.at[pl.ds(i * tall, tall)], got.at[i])
        for i in range(steps)
    ]
    for copy in copies:
        copy.start()
    return copies


def product(pieces, held, copies):
    left = jnp.concatenate([piece[...] for piece in pieces], axis=0)
    high, low = halves(left)
    both = jnp.concatenate([high, low], axis=0)
    m, tall = left.shape[0], held.shape[0] // len(copies)
    sums = jnp.zeros((m, held.shape[1]), jnp.float32)
    for i, copy in enumerate(copies):
        copy.wait()
        right_high, right_low = halves(held[i * tall : (i + 1) * tall, :])
        part = slice(i * tall, (i + 1) * tall)
        one = jnp.dot(both[:, part], right_high, preferred_element_type=jnp.float32)
        two = jnp.dot(high[:, part], right_low, preferred_element_type=jnp.float32)
        sums = sums + (one[:m] + one[m:] + two)
    return sums


def gram_kernel(masks, where_ref, *refs):
    pieces, panel_t, mine = refs[: len(masks)], refs[-2], refs[-1]
    col, row = where_ref[0], where_ref[1]
    width = pieces[0].shape[0]
    n = width * len(masks)
    for mask, piece in zip(masks, pieces):
        panel_t[pl.ds(pl.multiple_of((col ^ mask) * width, width), width), :] = piece[...]

    @pl.when(col & 1 == 0)
    def _():
        whole = panel_t[...]
        high = whole.astype(jnp.bfloat16)
        rest = whole - high.astype(jnp.float32)
        middle = rest.astype(jnp.bfloat16)
        low = (rest - middle.astype(jnp.float32)).astype(jnp.bfloat16)
        parts = lax.dot_general(
            jnp.concatenate([high, middle, low], axis=0),
            jnp.concatenate([high, middle], axis=0),
            (((1,), (1,)), ((), ())),
            preferred_element_type=jnp.float32,
        )
        small = parts[n : 2 * n, n:] + (parts[2 * n :, :n] + parts[2 * n :, :n].T)
        mine[...] = parts[:n, :n] + ((parts[n : 2 * n, :n] + parts[:n, n:]) + small)

    @pl.when(col & 1 == 1)
    def _():
        mine[...] = jnp.where(row == 0, panel_t[:, :n].T, 0.0)


def gram(where, held):
    width, rows = held[0].shape
    n = width * len(held)
    return pl.pallas_call(
        lambda *refs: gram_kernel(tuple(held), *refs),
        out_shape=(jax.ShapeDtypeStruct((n, rows), jnp.float32), jax.ShapeDtypeStruct((n, n), jnp.float32)),
        in_specs=[SCALAR] + [WHOLE] * len(held),
        compiler_params=pltpu.CompilerParams(vmem_limit_bytes=8 << 20),
        cost_estimate=FREE,
        name="gram",
    )(where, *held.values())


def copy_kernel(x, out):
    out[...] = x[...]


def nearby(x):
    return pl.pallas_call(
        copy_kernel,
        out_shape=jax.ShapeDtypeStruct(x.shape, x.dtype),
        in_specs=[WHOLE],
        compiler_params=pltpu.CompilerParams(vmem_limit_bytes=1 << 20),
        cost_estimate=FREE,
        name="nearby",
    )(x)


def products_kernel(where_ref, panel_t, trailing, keep, give, left, held, got):
    copies = fetch(trailing, held, got)
    n, rows = panel_t.shape

    @pl.when(where_ref[1] >= 0)
    def _():
        for i in range(0, rows, n):
            left[i : i + n, :n], left[i : i + n, n:] = halves(panel_t[:, i : i + n].T)
        sums = product([panel_t], held, copies)
        half = sums.shape[1] // 2
        first = where_ref[1] & 1 == 0
        keep[...] = jnp.where(first, sums[:, :half], sums[:, half:])
        give[...] = jnp.where(first, sums[:, half:], sums[:, :half])


def products_of(where, panel_t, trailing):
    (n, rows), cols = panel_t.shape, trailing.shape[1]
    part = jax.ShapeDtypeStruct((n, cols // 2), jnp.float32)
    return pl.pallas_call(
        products_kernel,
        out_shape=(part, part, jax.ShapeDtypeStruct((rows, 2 * n), jnp.bfloat16)),
        in_specs=[SCALAR, WHOLE, anywhere()],
        scratch_shapes=[pltpu.VMEM(trailing.shape, jnp.float32), pltpu.SemaphoreType.DMA((8,))],
        compiler_params=pltpu.CompilerParams(vmem_limit_bytes=MOST),
        cost_estimate=pl.CostEstimate(flops=0, bytes_accessed=11_000_000, transcendentals=0),
        name="products",
    )(where, panel_t, trailing)


def update_kernel(pieces, second, where_ref, left_ref, trailing, *refs):
    mixed, refs = refs[: len(pieces)], refs[len(pieces) :]
    if second:
        top_ref, _, updated, high_ref, low_ref, result, sent = refs
    else:
        pivot, replaced, updated, reflectors, top_ref, high_ref, low_ref, result, sent = refs
    row = where_ref[1]
    n, width = mixed[0].shape
    steps, tall = result.shape[0], result.shape[1]
    mine = 1 - (row & 1) if second else row & 1
    first_piece = pl.multiple_of(mine * (PIECES * width) + pieces[0] * width, width)
    columns = pl.ds(first_piece, len(pieces) * width)

    def going(i):
        return pltpu.make_async_copy(result.at[i], updated.at[pl.ds(i * tall, tall), columns], sent.at[i])

    if not second:
        top_ref[...] = jnp.where(row == 0, jnp.concatenate(halves(replaced[...]), axis=1), left_ref[:n, :])
    high, low = halves(jnp.concatenate([piece[...] for piece in mixed], axis=1))
    high_ref[:n], high_ref[n:] = high, high
    low_ref[:n], low_ref[n:] = low, low

    def rows_of(i):
        left = left_ref[i * tall : (i + 1) * tall, :]
        return jnp.concatenate([top_ref[...], left[n:]], axis=0) if i == 0 else left

    def times(left, high, low):
        return jnp.dot(left, high, preferred_element_type=jnp.float32) + jnp.dot(
            left, low, preferred_element_type=jnp.float32
        )

    for first in range(0, steps, 2):
        @pl.when(row >= 0)
        def _():
            for i in range(first, first + 2):
                change = times(rows_of(i), high_ref[...], low_ref[...])
                result[i] = trailing[i * tall : (i + 1) * tall, columns] - change
                going(i).start()

    if not second:
        width = reflectors.shape[0]
        own = pltpu.roll(pivot[...], (n - where_ref[0] * width) % n, 1)
        a, b = halves(own)
        a, b = jnp.concatenate([a, a], axis=0), jnp.concatenate([b, b], axis=0)
        for i in range(steps):
            reflectors[:, i * tall : (i + 1) * tall] = times(rows_of(i), a, b).T[:width]
    for i in range(steps):
        going(i).wait()


def update_call(pieces, second, where, left, trailing, mixed, inputs, outs, specs, name, aliases):
    n, width = mixed[0].shape
    width *= len(pieces)
    rows, steps = trailing.shape[0], 8
    return pl.pallas_call(
        lambda *refs: update_kernel(pieces, second, *refs),
        out_shape=outs,
        in_specs=[SCALAR, WHOLE, WHOLE] + [WHOLE] * len(pieces) + specs,
        out_specs=(anywhere(),) + (WHOLE,) * (len(outs) - 1),
        scratch_shapes=[pltpu.VMEM((2 * n, width), jnp.bfloat16)] * 2
        + [pltpu.VMEM((steps, rows // steps, width), jnp.float32)]
        + [pltpu.SemaphoreType.DMA((steps,))],
        input_output_aliases=aliases,
        compiler_params=pltpu.CompilerParams(vmem_limit_bytes=8 << 20),
        cost_estimate=FREE,
        name=name,
    )(where, left, trailing, *mixed, *inputs)


def update(where, left, mixed, trailing, pivot, replaced, width):
    n, rows = mixed[0].shape[0], trailing.shape[0]
    outs = (
        jax.ShapeDtypeStruct(trailing.shape, jnp.float32),
        jax.ShapeDtypeStruct((width, rows), jnp.float32),
        jax.ShapeDtypeStruct((n, 2 * n), jnp.bfloat16),
    )
    pieces = tuple(range(PIECES))
    return update_call(
        pieces, False, where, left, trailing, mixed, (pivot, replaced), outs, [WHOLE, WHOLE], "update", {}
    )


def update_rest(piece, where, left, top, mixed, trailing, updated):
    outs = (jax.ShapeDtypeStruct(trailing.shape, jnp.float32),)
    inputs = (top, updated)
    return update_call(
        (piece,), True, where, left, trailing, (mixed,), inputs, outs, [WHOLE, anywhere()], "update_rest", {5: 0}
    )[0]


def mix(mine, theirs, lead, inv):
    def kernel(mine, theirs, lead, inv, *outs):
        right = jnp.concatenate([lead[...], mine[...] + theirs[...]], axis=0)
        mixed = dot(inv[...], right, (1, 0))
        width = outs[0].shape[1]
        for i, out in enumerate(outs):
            out[...] = mixed[:, i * width : (i + 1) * width]

    n, half = mine.shape
    return pl.pallas_call(
        kernel,
        out_shape=(jax.ShapeDtypeStruct((n, half // PIECES), jnp.float32),) * PIECES,
        in_specs=[WHOLE] * 4,
        compiler_params=pltpu.CompilerParams(vmem_limit_bytes=3 << 20),
        cost_estimate=FREE,
        name="mix",
    )(mine, theirs, lead, inv)


def after(x, *others):
    return lax.optimization_barrier((x, *others))[0]


def per_device(panel_block, trailing):
    own = panel_block.T
    col, row = lax.axis_index("col"), lax.axis_index("row")
    where = jnp.stack([col, row]).astype(jnp.int32)
    held = {0: own}
    for bit in reversed(bits_of("col")):
        if bit == 1:
            far = max(held)
            own, held[1] = lax.optimization_barrier((own, swap(own, "col", 1)))
            held[0], held[far] = lax.optimization_barrier((nearby(own), held[far]))
        held.update({m | bit: swap(piece, "col", bit) for m, piece in list(held.items()) if m | bit not in held})
    n = own.shape[0] * len(held)
    bits = bits_of("row")
    mirrored = sum(bits[1:])
    odd, half = row & bits[0] != 0, trailing.shape[1] // 2

    lead, _ = lax.optimization_barrier((trailing[:n], held[1]))
    keep, give = lax.optimization_barrier(
        (lead[:, :half], jnp.where(odd, lead[:, :half], lead[:, half:]))
    )
    lead = jnp.where(odd, swap(give, "row", bits[0]), keep)
    for bit in bits[1:-1]:
        lead = jnp.where(row & bit != 0, swap(lead, "row", bit), lead)
    panel_t, mine = gram(where, held)
    keep, give, left = products_of(where, panel_t, trailing)
    got = swap(give, "row", bits[0])
    for bit in bits[1:-1]:
        mine = mine + lax.optimization_barrier((swap(mine, "row", bit), keep))[0]
    lead, mine = lax.optimization_barrier((lead, mine))
    got_z = swap(mine, "row", mirrored)
    mine = mine + got_z
    sums, lead, mine = lax.optimization_barrier((keep + got, lead, mine))
    lead_got = swap(lead, "row", bits[-1])
    mine = mine + swap(mine, "row", bits[0])
    for bit in bits[1:-1]:
        sums = sums + swap(sums, "row", bit)
    theirs = swap(mine, "col", 1)
    last = swap(sums, "row", mirrored)
    theirs, sums = lax.optimization_barrier((theirs, sums))
    lead = jnp.where(row & bits[-1] != 0, lead_got, lead)
    odd_col = col.astype(jnp.int32).reshape(1) & 1
    panel_factor, inv, pivot, replaced, kept = factor(odd_col, mine, theirs, trailing)
    mixed = mix(sums, last, lead, inv)
    others = [swap(piece, "row", bits[0]) for piece in mixed]
    updated, reflectors, top = update(where, left, mixed, kept, pivot, replaced, own.shape[0])
    for i, other in enumerate(others):
        updated = update_rest(i, where, left, top, other, kept, updated)
    return updated, reflectors.T, panel_factor


def solution(mesh):
    in_specs = (P("row", "col"), P("row", "col"))
    out_specs = (P("row", "col"), P("row", "col"), P())
    return jax.shard_map(per_device, mesh=mesh, in_specs=in_specs, out_specs=out_specs, check_vma=False)
```
